256 devices in a mesh: band: 8 (over y, core), tile: 32 (over z, x).
Axes of the slice: x: 4, y: 4, z: 8, core: 2. Of those that a mesh axis runs over, the one named last changes fastest.
Arguments:
- right_side: float32 [16, 192, 4096], P(None, 'band', 'tile'), may hold values from -54 to 54
- coeff_field: float32 [192, 4096], P('band', 'tile'), may hold values from 0.25 to 4
- factor_blocks: bfloat16 [8, 32, 116, 128, 128], P('band', 'tile'), may hold values from -1 to 2, as said below
- block_rows: int32 [8, 32, 116], P('band', 'tile'), may hold values from 0 to 28, as said below
- block_cols: int32 [8, 32, 116], P('band', 'tile'), may hold values from 0 to 28, as said below
- prolong: float32 [192, 1, 128, 4096], P('band', None, None, 'tile'), may hold values from -0.3125 to 0.3125
- coarse_picks: int32 [192, 32, 1], P('band', 'tile'), may hold values from 0 to 3
- coarse_factor: float32 [8, 512, 512], P('band'), may hold values from -1 to 1, as said below
Outputs:
- solution: float32 [16, 192, 4096], P(None, 'band', 'tile')
- residual: float32 [16, 192, 4096], P(None, 'band', 'tile')
- precond: float32 [16, 192, 4096], P(None, 'band', 'tile')
The draws below stay inside these ranges and needn't reach their ends.
Inputs may be any that keep to these rules, and one draw needn't show every extreme that they name: `block_rows`: entry k < 29 of a subdomain's list is k; every later entry is a tile row of 1 to 28. `block_cols`: entry k < 29 is k, so that tile (k, k) is stored first; every later entry is below its block_rows entry. `factor_blocks`: stored tile k < 29 of a subdomain is its diagonal tile: lower triangular with diagonal entries of 1 to 2. `coarse_factor`: lower triangular, diagonal entries of 0.6 to 1.0. `coarse_picks`: the 1 slots of a row name different blocks.
All inputs are finite; a program needn't handle non-finite values.
Results may differ from the reference program's by a relative error of at most 0.018.
Values may be sent and summed in bfloat16 or wider, within the bound.
A program may use at most 64 MiB of HBM per device.

```python
import math
import jax
import jax.numpy as jnp
from jax import lax

COLS = 16
LAT = 24
LON = 128
W = 2
TILE_N = 128
CN = 512
NCB = 4
CB = 1
ITERS = 3
CBS = 128
K = 29
NB = 116
NLAT = 192
NLON = 4096
N_BAND = 8
N_TILE = 32


def block_pairs(key):
    draw_shape = (N_BAND, N_TILE, NB - K)
    row_tiles = jax.random.randint(jax.random.fold_in(key, 101), draw_shape, 1, K)
    spare_bits = jax.random.randint(jax.random.fold_in(key, 102), draw_shape, 0, 1048576)
    col_tiles = spare_bits % row_tiles
    diagonal = jnp.broadcast_to(jnp.arange(K, dtype=jnp.int32), (N_BAND, N_TILE, K))
    rows_all = jnp.concatenate([diagonal, row_tiles.astype(jnp.int32)], axis=-1)
    cols_all = jnp.concatenate([diagonal, col_tiles.astype(jnp.int32)], axis=-1)
    return (rows_all, cols_all)


def draw_block_rows(key, part):
    paired = block_pairs(key)
    return paired[0]


def draw_block_cols(key, part):
    paired = block_pairs(key)
    return paired[1]


def noise_draw(key, draw_shape):
    return jnp.clip(jax.random.normal(key, draw_shape, jnp.float32), -4.0, 4.0)


def draw_factor_blocks(key, part):
    key = jax.random.fold_in(key, 5)
    draw_shape = (N_BAND, N_TILE, NB, TILE_N, TILE_N)
    noise = noise_draw(jax.random.fold_in(key, 1), draw_shape)
    diag_values = jax.random.uniform(jax.random.fold_in(key, 2), (N_BAND, N_TILE, NB, TILE_N), jnp.float32, 1.0, 2.0)
    index_row = jnp.arange(TILE_N, dtype=jnp.int32)[:, None]
    index_col = jnp.arange(TILE_N, dtype=jnp.int32)[None, :]
    scaled = noise / math.sqrt(TILE_N)
    diag_block = jnp.where(index_row == index_col, diag_values[..., None], jnp.where(index_row > index_col, 0.5 * scaled, 0.0))
    is_diagonal = (jnp.arange(NB, dtype=jnp.int32) < K)[:, None, None]
    return jnp.where(is_diagonal, diag_block, 0.5 * scaled).astype(jnp.bfloat16)


def draw_coarse_factor(key, part):
    key = jax.random.fold_in(key, 7)
    draw_shape = (N_BAND, CN, CN)
    noise = noise_draw(jax.random.fold_in(key, 1), draw_shape)
    diag_values = jax.random.uniform(jax.random.fold_in(key, 2), (N_BAND, CN), jnp.float32, 0.6, 1.0)
    index_row = jnp.arange(CN, dtype=jnp.int32)[:, None]
    index_col = jnp.arange(CN, dtype=jnp.int32)[None, :]
    lower_part = jnp.where(index_row > index_col, 0.3 * noise / math.sqrt(CN), 0.0)
    return jnp.where(index_row == index_col, diag_values[..., None], lower_part).astype(jnp.float32)


def draw_right_side(key, part):
    key = jax.random.fold_in(key, 9)
    draw_shape = (COLS, NLAT, NLON)
    lat_frac = jnp.arange(NLAT, dtype=jnp.float32) / NLAT
    lon_frac = jnp.arange(NLON, dtype=jnp.float32) / NLON
    scale = jnp.exp(math.log(3.0) * (lat_frac[:, None] + lon_frac[None, :]))
    noise = jnp.clip(jax.random.normal(jax.random.fold_in(key, 1), draw_shape, jnp.float32), -6.0, 6.0)
    values = noise * scale[None]
    return jnp.clip(values, -54.0, 54.0).astype(jnp.float32)


def block_levels(stream_key, shape, cuts, low, high):
    loudness, own = 1.0, jax.random.fold_in(stream_key, 6)
    for axis_at, parts in cuts:
        steps = jnp.exp(jax.random.uniform(jax.random.fold_in(own, axis_at), (parts,), jnp.float32, low / len(cuts), high / len(cuts)))
        loudness = loudness * jnp.repeat(steps, shape[axis_at] // parts).reshape([-1 if axis == axis_at else 1 for axis in range(len(shape))])
    return loudness


def different_ones(key, rows, count, top, lift):
    ranking = jax.random.permutation(jax.random.fold_in(key, 1), count)
    pull = ranking
    for power in range(3):
        pull = pull * pull // count
    pull = pull * lift // count
    tickets = jax.random.randint(jax.random.fold_in(key, 2), (rows, count), 0, 4096) + pull
    fixed_rows = jax.random.permutation(jax.random.fold_in(key, 3), rows)[jnp.arange(count) % rows]
    tickets = jnp.where(jnp.arange(rows)[:, None] == fixed_rows[None, :], 1 << 14, tickets)
    priority = tickets * count + jnp.arange(count)
    return lax.top_k(priority.astype(jnp.int32), top)[1].astype(jnp.int32)


def bell_draw(own_key, extent, scale, reach, shards=(), kind=jnp.bfloat16):
    result = scale * jax.random.normal(own_key, extent, jnp.float32)
    if shards:
        result = result * block_levels(own_key, extent, shards, -0.22, 0.18)
    return jnp.clip(result, -reach, reach).astype(kind)


def setup_inputs(seed: int = 0) -> dict:
    key_list = jax.random.split(jax.random.key(seed), 9)
    return {
        "right_side": draw_right_side(jax.random.fold_in(key_list[8], 71), 0),
        "coeff_field": jnp.clip(jnp.exp(math.log(4.0) - 2.7725887 * jax.random.uniform(key_list[1], (NLAT, NLON), jnp.float32) ** block_levels(key_list[1], (NLAT, NLON), ((0, 8), (1, 32)), -0.2, 0.2)), 0.25, 4.0),
        "factor_blocks": draw_factor_blocks(jax.random.fold_in(key_list[8], 71), 0),
        "block_rows": draw_block_rows(jax.random.fold_in(key_list[8], 71), 0),
        "block_cols": draw_block_cols(jax.random.fold_in(key_list[8], 71), 0),
        "prolong": bell_draw(key_list[5], (NLAT, CB, CBS, NLON), (3 * CB * CBS) ** -0.5, 0.3125, ((0, 8), (3, 32)), jnp.float32),
        "coarse_picks": different_ones(key_list[6], NLAT * N_TILE, NCB, CB, 0).reshape((NLAT, N_TILE, CB)),
        "coarse_factor": draw_coarse_factor(jax.random.fold_in(key_list[8], 71), 0),
    }


highest = lax.Precision.HIGHEST


def stencil(padded, coeff):
    center = padded[:, 1:-1, 1:-1]
    beside_all = padded[:, :-2, 1:-1] + padded[:, 2:, 1:-1] + padded[:, 1:-1, :-2] + padded[:, 1:-1, 2:]
    return 0.25 * ((coeff + 4.0) * center - beside_all)


def operator_apply(field, coeff):
    first_k = stencil(jnp.pad(field, ((0, 0), (1, 1), (1, 1))), coeff)
    return stencil(jnp.pad(first_k, ((0, 0), (1, 1), (1, 1))), coeff)


def block_solve(extended, factor, rows_idx, cols_idx):
    columns, ext_rows, ext_cols = extended.shape
    node_count = ext_rows * ext_cols
    tile_size = factor.shape[-1]
    block_count = factor.shape[0]
    tile_count = (node_count + tile_size - 1) // tile_size
    flattened = jnp.pad(extended.reshape(columns, node_count), ((0, 0), (0, tile_count * tile_size - node_count)))
    pieces = flattened.astype(jnp.bfloat16).reshape(columns, tile_count, tile_size).transpose(1, 0, 2)
    places = jnp.arange(tile_count, dtype=jnp.int32)[:, None]
    place_rows = (rows_idx[None, :] == places).astype(jnp.float32)
    place_cols = (cols_idx[None, :] == places).astype(jnp.float32)
    inner_part = jnp.einsum("bij,bcj->bci", factor.astype(jnp.float32), pieces[cols_idx].astype(jnp.float32), precision=highest)
    gathered = jnp.dot(place_rows, inner_part.reshape(block_count, -1), precision=highest)
    gathered = gathered.astype(jnp.bfloat16).reshape(tile_count, columns, tile_size)
    outer_part = jnp.einsum("bij,bci->bcj", factor.astype(jnp.float32), gathered[rows_idx].astype(jnp.float32), precision=highest)
    spread = jnp.dot(place_cols, outer_part.reshape(block_count, -1), precision=highest)
    spread = spread.reshape(tile_count, columns, tile_size).transpose(1, 0, 2).reshape(columns, tile_count * tile_size)
    return spread[:, :node_count].reshape(columns, ext_rows, ext_cols)


def schwarz(field, factor_blocks, block_rows, block_cols):
    columns = field.shape[0]
    ext_rows = LAT + 2 * W
    ext_cols = LON + 2 * W
    padded = jnp.pad(field, ((0, 0), (W, W), (W, W)))

    def visit_one(summed, position):
        band_at = position // N_TILE
        tile_at = position % N_TILE
        anchor = jnp.zeros((), jnp.int32)
        starts = (anchor, (band_at * LAT).astype(jnp.int32), (tile_at * LON).astype(jnp.int32))
        extended = lax.dynamic_slice(padded, starts, (columns, ext_rows, ext_cols))
        spread = block_solve(extended, factor_blocks[band_at, tile_at], block_rows[band_at, tile_at], block_cols[band_at, tile_at])
        current = lax.dynamic_slice(summed, starts, (columns, ext_rows, ext_cols))
        return lax.dynamic_update_slice(summed, current + spread, starts), None

    summed, unused = lax.scan(visit_one, jnp.zeros(padded.shape, jnp.float32), jnp.arange(N_BAND * N_TILE, dtype=jnp.int32))
    return summed[:, W:W + NLAT, W:W + NLON]


def coarse_tables(prolong, coarse_picks):
    blocks_p = prolong.reshape(N_BAND, LAT, CB, CBS, N_TILE, LON)
    choose = (coarse_picks.reshape(N_BAND, LAT, N_TILE, CB)[..., None] == jnp.arange(NCB, dtype=jnp.int32)).astype(jnp.float32)
    return blocks_p, choose


def coarse_restrict(field, blocks_p, choose):
    columns = field.shape[0]
    split = field.reshape(columns, N_BAND, LAT, N_TILE, LON)
    partial_value = jnp.einsum("brkstl,cbrtl->cbrtks", blocks_p, split, precision=highest)
    coarse = jnp.einsum("cbrtks,brtkn->bcns", partial_value, choose, precision=highest)
    return coarse.reshape(N_BAND, columns, CN)


def coarse_solve(coarse_in, coarse_factor):
    halfway = jnp.einsum("bcn,bmn->bcm", coarse_in, coarse_factor, precision=highest)
    return jnp.einsum("bcm,bmn->bcn", halfway, coarse_factor, precision=highest)


def coarse_lift(solved, blocks_p, choose):
    columns = solved.shape[1]
    picked = jnp.einsum("brtkn,bcns->cbrtks", choose, solved.reshape(N_BAND, columns, NCB, CBS), precision=highest)
    lifted = jnp.einsum("brkstl,cbrtks->cbrtl", blocks_p, picked, precision=highest)
    return lifted.reshape(columns, NLAT, NLON)


def reference(right_side, coeff_field, factor_blocks, block_rows, block_cols, prolong, coarse_picks, coarse_factor):
    blocks_p, choose = coarse_tables(prolong, coarse_picks)

    def precondition(field):
        local_part = schwarz(field, factor_blocks, block_rows, block_cols)
        solved = coarse_solve(coarse_restrict(field, blocks_p, choose), coarse_factor)
        return local_part + coarse_lift(solved, blocks_p, choose)

    solution = jnp.zeros_like(right_side)
    residual = right_side
    precond = precondition(residual)
    precond_dot = jnp.sum(residual * precond, axis=(1, 2))
    search = precond
    for iteration in range(ITERS):
        image = operator_apply(search, coeff_field)
        step_size = precond_dot / jnp.sum(search * image, axis=(1, 2))
        solution = solution + step_size[:, None, None] * search
        residual = residual - step_size[:, None, None] * image
        precond = precondition(residual)
        if iteration + 1 < ITERS:
            dot_next = jnp.sum(residual * precond, axis=(1, 2))
            search = precond + (dot_next / precond_dot)[:, None, None] * search
            precond_dot = dot_next
    return solution, residual, precond
```

```python
import functools

import jax
import jax.numpy as jnp
from jax import lax
from jax.experimental import pallas as pl
from jax.experimental.pallas import tpu as pltpu
from jax.sharding import PartitionSpec as P

MESH = pl.DeviceIdType.MESH
W = 2
NCB = 4
ITERS = 3
STAGES = ITERS + 1
M4 = 4
F32 = jnp.float32
BF16 = jnp.bfloat16


def loop(count, body, init=None, unroll=1):
    if init is None:

        def step(i, carry):
            body(i)
            return carry

        return lax.fori_loop(0, count, step, 0, unroll=unroll)
    return lax.fori_loop(0, count, body, init, unroll=unroll)


def dot_nn(a, b):
    return lax.dot_general(a, b, (((1,), (0,)), ((), ())), preferred_element_type=F32)


def dot_nt(a, b):
    return lax.dot_general(a, b, (((1,), (1,)), ((), ())), preferred_element_type=F32)


def halves(value):
    high = value.astype(BF16)
    low = (value - high.astype(F32)).astype(BF16)
    return jnp.concatenate([high, low], axis=0)


def kernel(
    cfg,
    tab,
    rs_hbm,
    co_hbm,
    f_hbm,
    p_hbm,
    c_hbm,
    x_out,
    r_out,
    u_out,
    rs,
    co,
    fac,
    pf,
    cf,
    pb,
    pb2,
    bmat,
    bmat2,
    zcat,
    iVO,
    iVH,
    isb,
    irb,
    VO,
    VH,
    LVO,
    LVH,
    sb,
    rb,
    UO,
    UH,
    AO,
    AH,
    FO,
    FH,
    c4O,
    c4H,
    lO,
    lH,
    lsO,
    lsH,
    TO,
    TH,
    S,
    Pp,
    y,
    ys,
    yw,
    xin,
    gin,
    run,
    prev,
    qa,
    qar,
    qb,
    qbr,
    da,
    dar,
    db,
    dbr,
    insem,
    exsem_s,
    exsem_r,
    qasem_s,
    qasem_r,
    qbsem_s,
    qbsem_r,
    dasem_s,
    dasem_r,
    dbsem_s,
    dbsem_r,
):
    n_b, n_t, nx, nz, lat, nb_blocks, kt, cols = cfg
    b = lax.axis_index("band")
    t = lax.axis_index("tile")
    z = t // nx
    x = t % nx
    own = lat
    ext = lat + 2 * W
    full = lat + 2 * M4

    loads = [
        pltpu.make_async_copy(rs_hbm, rs, insem.at[0]),
        pltpu.make_async_copy(co_hbm, co, insem.at[1]),
        pltpu.make_async_copy(p_hbm, pf, insem.at[2]),
        pltpu.make_async_copy(c_hbm, cf, insem.at[3]),
        pltpu.make_async_copy(f_hbm, fac, insem.at[4]),
    ]
    for copy in loads:
        copy.start()

    def band_at(d):
        return lax.rem(b + d + n_b, n_b)

    def tile_at(d):
        return lax.rem(t + d + n_t, n_t)

    def x_peer(d):
        return (b, z * nx + lax.rem(x + d, nx))

    def z_peer(d):
        return (b, lax.rem(t + nx * d, n_t))

    def plane_peer(d):
        return (lax.rem(b + d // nx, n_b), z * nx + lax.rem(x + lax.rem(d, nx), nx))

    n_plane = n_b * nx - 1
    barrier = pltpu.get_barrier_semaphore()

    def greet(device):
        pl.semaphore_signal(barrier, inc=1, device_id=device, device_id_type=MESH)

    loop(n_plane, lambda d: greet(plane_peer(d + 1)))
    loop(nz - 1, lambda d: greet(z_peer(d + 1)))
    for db_ in (-1, 0, 1):
        for dt_ in (-1, 1):
            greet((band_at(db_), tile_at(dt_)))
    pl.semaphore_wait(barrier, n_plane + nz - 1 + 6)

    has_n = (b > 0).astype(F32)
    has_s = (b < n_b - 1).astype(F32)
    has_w = (t > 0).astype(F32)
    has_e = (t < n_t - 1).astype(F32)

    def lane_of(rows):
        return lax.broadcasted_iota(jnp.int32, (rows, 128), 1)

    def pack_send(vO, vH, sbe, rbe, ssem, rsem):
        rows = vO.shape[1]
        lane = lane_of(rows)
        west_half = lane >= 64
        group = lane // 8
        zero = jnp.zeros((rows, 128), F32)

        def half(first_slot, first_row):
            def body(n, carry):
                tw, te = carry
                slot = first_slot + n
                row = first_row + n
                o = vO[row]
                h = vH[row]
                shift = lax.rem(8 * slot + 4, 128)
                here = group == slot
                w = pltpu.roll(jnp.where(west_half, h, o), shift, 1)
                e = pltpu.roll(jnp.where(west_half, o, h), shift, 1)
                return tw + jnp.where(here, w, 0.0), te + jnp.where(here, e, 0.0)

            return loop(ext // 2, body, (zero, zero), unroll=ext // 2)

        tw0, te0 = half(2, 0)
        tw1, te1 = half(0, ext // 2)
        for n in range(6):
            sbe[n] = vO[n]
            sbe[8 + n] = vO[ext - 6 + n]
        sbe[6] = tw0
        sbe[7] = te0
        sbe[14] = tw1
        sbe[15] = te1
        sbe[16] = te0
        sbe[17] = te1
        sbe[18] = tw0
        sbe[19] = tw1
        for first, count, to, db_, dt_ in (
            (0, 8, 8, -1, 0),
            (8, 8, 0, 1, 0),
            (16, 2, 18, 0, 1),
            (18, 2, 16, 0, -1),
            (16, 1, 22, -1, 1),
            (17, 1, 20, 1, 1),
            (18, 1, 23, -1, -1),
            (19, 1, 21, 1, -1),
        ):
            pltpu.make_async_remote_copy(
                src_ref=sbe.at[pl.ds(first, count)],
                dst_ref=rbe.at[pl.ds(to, count)],
                send_sem=ssem,
                recv_sem=rsem,
                device_id=(band_at(db_), tile_at(dt_)),
                device_id_type=MESH,
            ).start()

    def assemble(vO, sbe, rbe, rsem, emit):
        rows = vO.shape[1]
        lane = lane_of(rows)
        pltpu.make_async_copy(rbe, rbe, rsem).wait()
        low = jnp.where(lane < 48, 1.0, 0.0)
        high = jnp.where(lane >= 80, 1.0, 0.0)
        m_w = jnp.where(lane >= 124, has_w, 0.0)
        m_e = jnp.where(lane < 4, has_e, 0.0)

        def turned(slot):
            return pltpu.roll(rbe[slot], 64, 1)

        pw = (
            sbe[18] + has_w * rbe[18] + (has_n * low) * (turned(6) + has_w * turned(20)),
            sbe[19] + has_w * rbe[19] + (has_s * high) * (turned(14) + has_w * turned(22)),
        )
        pe = (
            sbe[16] + has_e * rbe[16] + (has_n * low) * (turned(7) + has_e * turned(21)),
            sbe[17] + has_e * rbe[17] + (has_s * high) * (turned(15) + has_e * turned(23)),
        )

        def finish(o, slot, half, scale, i):
            shift = lax.rem(124 - 8 * slot + 128, 128)
            w = pltpu.roll(pw[half], shift, 1)
            e = pltpu.roll(pe[half], shift, 1)
            o = jnp.where(lane < 4, w, jnp.where(lane >= 124, e, o))
            h = w * m_w + e * m_e
            if scale is not None:
                o = o * scale
                h = h * scale
            emit(i, o, h)

        for i in range(6):
            o = has_n * rbe[i]
            if i >= 2:
                o = o + vO[i - 2]
            finish(o, i, 0, has_n if i < M4 else None, i)
        mid0 = 10
        mid1 = full - 6 - 16

        def body0(n):
            finish(vO[4 + n], 6 + n, 0, None, 6 + n)

        def body1(n):
            finish(vO[14 + n], n, 1, None, 16 + n)

        loop(mid0, body0, unroll=mid0)
        loop(mid1, body1, unroll=mid1)
        for n in range(6):
            i = full - 6 + n
            o = has_s * rbe[8 + n]
            if i < full - 2:
                o = o + vO[i - 2]
            finish(o, i - 16, 1, has_s if i >= full - M4 else None, i)

    def restrict_send(k):
        def body(row, acc):
            both = halves(FO[row + W])
            part = dot_nt(both, pb[row])
            part = part[0:cols] + part[cols:] + dot_nt(both[0:cols], pb2[row])
            pick = tab[8, row]
            return tuple(acc[m] + part * (pick == m).astype(F32) for m in range(NCB))

        zero = jnp.zeros((cols, 128), F32)
        acc = loop(own, body, (zero,) * NCB, unroll=own)
        for m in range(NCB):
            qa[k, m] = acc[m]

        def send(d):
            pltpu.make_async_remote_copy(
                src_ref=qa.at[k],
                dst_ref=qar.at[k, d],
                send_sem=qasem_s.at[k],
                recv_sem=qasem_r.at[k],
                device_id=x_peer(d + 1),
                device_id_type=MESH,
            ).start()

        for d in range(nx - 1):
            send(d)

    def dots_send(k, gamma, delta, eps):
        lane = lane_of(cols)
        g = jnp.sum(gamma, axis=1, keepdims=True)
        d = jnp.sum(delta, axis=1, keepdims=True)
        e = jnp.sum(eps, axis=1, keepdims=True)
        tile = (
            jnp.where(lane == 0, g, 0.0) + jnp.where(lane == 1, d, 0.0) + jnp.where(lane == 2, e, 0.0)
        )
        da[k] = tile[0:8] + pltpu.roll(tile[8:16], 64, 1)

        def send(d):
            pltpu.make_async_remote_copy(
                src_ref=da.at[k],
                dst_ref=dar.at[k, d],
                send_sem=dasem_s.at[k],
                recv_sem=dasem_r.at[k],
                device_id=plane_peer(d + 1),
                device_id_type=MESH,
            ).start()

        loop(n_plane, send)

    def reduce_mid(k):
        pltpu.make_async_copy(qar.at[k], qar.at[k], qasem_r.at[k]).wait()
        for m in range(NCB):
            total = qa[k, m]
            for d in range(nx - 1):
                total = total + qar[k, d, m]
            qb[k, m] = total.astype(BF16)

        def send_q(d):
            pltpu.make_async_remote_copy(
                src_ref=qb.at[k],
                dst_ref=qbr.at[k, d],
                send_sem=qbsem_s.at[k],
                recv_sem=qbsem_r.at[k],
                device_id=z_peer(d + 1),
                device_id_type=MESH,
            ).start()

        for d in range(nz - 1):
            send_q(d)

    def dots_mid(k):
        pltpu.make_async_copy(dar.at[k], dar.at[k], dasem_r.at[k]).wait()
        total = da[k]
        for d in range(n_plane):
            total = total + dar[k, d]
        db[k] = total

        def send_d(d):
            pltpu.make_async_remote_copy(
                src_ref=db.at[k],
                dst_ref=dbr.at[k, d],
                send_sem=dbsem_s.at[k],
                recv_sem=dbsem_r.at[k],
                device_id=z_peer(d + 1),
                device_id_type=MESH,
            ).start()

        for d in range(nz - 1):
            send_d(d)

    def reduce_end(k):
        pltpu.make_async_copy(qbr.at[k], qbr.at[k], qbsem_r.at[k]).wait()
        for m in range(NCB):
            total = qb[k, m].astype(F32)
            for d in range(nz - 1):
                total = total + qbr[k, d, m].astype(F32)
            yw[m] = total

    def dots_end(k):
        pltpu.make_async_copy(dbr.at[k], dbr.at[k], dbsem_r.at[k]).wait()
        total = db[k]
        for d in range(nz - 1):
            total = total + dbr[k, d]
        tile = jnp.concatenate([total, pltpu.roll(total, 64, 1)], axis=0)
        shape = (cols, 128)
        return tuple(jnp.broadcast_to(tile[:, n : n + 1], shape) for n in range(3))

    def local_solve():
        lane = lane_of(cols)
        zero = jnp.zeros((cols, 128), F32)

        def flatten(j, carry):
            s = 4 * j + W
            o = pltpu.roll(FO[j], s, 1)
            h = pltpu.roll(FH[j], s, 1)
            late = lane >= s
            xin[j] = (jnp.where(late, o, h) + carry).astype(BF16)
            return jnp.where(late, h, o)

        tail = loop(ext, flatten, zero, unroll=ext)
        xin[ext] = tail.astype(BF16)

        def inner(n, acc):
            acc = acc * tab[2, n].astype(F32) + dot_nt(xin[tab[1, n]], fac[tab[0, n]])
            run[n] = acc
            return acc

        loop(nb_blocks, inner, zero, unroll=nb_blocks)

        def gather(i):
            gin[i] = run[tab[3, i]].astype(BF16)

        loop(kt, gather, unroll=kt)

        def outer(n, acc):
            acc = acc * tab[6, n].astype(F32) + dot_nn(gin[tab[5, n]], fac[tab[4, n]])
            run[n] = acc
            return acc

        loop(nb_blocks, outer, zero, unroll=nb_blocks)

        def unflatten(j, carry):
            s = 4 * j + W
            following = run[tab[7, j + 1]]
            here = pltpu.roll(carry, 128 - s, 1)
            there = pltpu.roll(following, 128 - s, 1)
            VO[j] = jnp.where(lane < 128 - s, here, there)
            VH[j] = jnp.where(lane >= 126, here, jnp.where(lane < 2, there, 0.0))
            return following

        loop(ext, unflatten, run[tab[7, 0]], unroll=ext)

    def near(value):
        lane = lane_of(cols)
        return jnp.where((lane < W) | (lane >= 128 - W), value, 0.0)

    rows24 = cols + 8
    zero24 = jnp.zeros((rows24, 128), F32)
    for row in (0, 1, ext - 2, ext - 1):
        iVO[row] = zero24
        LVO[row] = zero24[0:cols]
    iVH[...] = jnp.zeros(iVH.shape, F32)
    LVH[...] = jnp.zeros(LVH.shape, F32)
    for ref in (lO, lH, lsO, lsH, S, Pp, y, ys):
        ref[...] = jnp.zeros(ref.shape, F32)
    prev[...] = jnp.ones(prev.shape, F32)

    loads[0].wait()
    loads[1].wait()
    for row in range(own):
        value = rs[:, row, :]
        r_out[row] = value
        x_out[row] = jnp.zeros((cols, 128), F32)
        iVO[W + row, 0:cols] = value
        iVO[W + row, cols:rows24] = jnp.broadcast_to(co[row : row + 1, :], (8, 128))
    pack_send(iVO, iVH, isb, irb, exsem_s.at[0], exsem_r.at[0])

    def first_rows(row):
        FO[row + W] = r_out[row]

    loop(own, first_rows, unroll=own)
    loads[2].wait()

    def to_bf16(row):
        value = pf[row]
        high = value.astype(BF16)
        pb[row] = high
        pb2[row] = (value - high.astype(F32)).astype(BF16)

    loop(own, to_bf16, unroll=4)
    restrict_send(0)
    loads[3].wait()
    for m in range(NCB):
        value = lax.dot_general(
            cf[:, m * 128 : (m + 1) * 128],
            cf[...],
            (((0,), (0,)), ((), ())),
            precision=lax.Precision.HIGHEST,
            preferred_element_type=F32,
        )
        high = value.astype(BF16)
        bmat[m * 128 : (m + 1) * 128, :] = high
        bmat2[m * 128 : (m + 1) * 128, :] = (value - high.astype(F32)).astype(BF16)

    lane16 = lane_of(cols)

    def take_first(i, o, h):
        if isinstance(i, int):
            keep = W <= i < full - W
        else:
            keep = True
        if keep:
            FO[i - W] = o[0:cols]
            FH[i - W] = near(h[0:cols])
        inside = 0.25
        if isinstance(i, int):
            if i < M4:
                inside = 0.25 * has_n
            elif i >= full - M4:
                inside = 0.25 * has_s
        lane8 = lane16[0:8]
        side = jnp.where(lane8 >= 128 - M4, has_w, 0.0) + jnp.where(lane8 < M4, has_e, 0.0)
        c4O[i] = (o[cols:rows24] + 4.0) * inside
        c4H[i] = (h[cols:rows24] + 4.0) * (side * inside)

    assemble(iVO, isb, irb, exsem_r.at[0], take_first)
    loads[4].wait()

    side16 = jnp.where(lane16 >= 128 - M4, has_w, 0.0) + jnp.where(lane16 < M4, has_e, 0.0)
    last_lane = lane16 == 127
    first_lane = lane16 == 0

    def row_scale(i):
        north = jnp.where(i < M4, has_n, 1.0)
        south = jnp.where(i >= full - M4, has_s, 1.0)
        return 0.25 * north * south

    def apply_row(srcO, srcH, i):
        o = srcO[i]
        h = srcH[i]
        ol = pltpu.roll(o, 1, 1)
        hl = pltpu.roll(h, 1, 1)
        orr = pltpu.roll(o, 127, 1)
        hr = pltpu.roll(h, 127, 1)
        around_o = (
            srcO[i - 1]
            + srcO[i + 1]
            + jnp.where(first_lane, hl, ol)
            + jnp.where(last_lane, hr, orr)
        )
        around_h = (
            srcH[i - 1]
            + srcH[i + 1]
            + jnp.where(first_lane, ol, hl)
            + jnp.where(last_lane, orr, hr)
        )
        scale = row_scale(i)
        co_ = jnp.concatenate([c4O[i], c4O[i]], axis=0)
        ch_ = jnp.concatenate([c4H[i], c4H[i]], axis=0)
        return co_ * o - scale * around_o, ch_ * h - (scale * side16) * around_h

    def stage(k, carry):
        local_solve()
        pack_send(VO, VH, sb.at[k], rb.at[k], exsem_s.at[1 + k], exsem_r.at[1 + k])
        reduce_mid(k)

        @pl.when(k > 0)
        def _():
            dots_mid(k)

        def keep(i, o, h):
            TO[i] = o
            TH[i] = h

        assemble(VO, sb.at[k], rb.at[k], exsem_r.at[1 + k], keep)
        reduce_end(k)

        @pl.when(k > 0)
        def _():
            g, d, e = dots_end(k)
            beta = jnp.where(k > 1, g / prev[0], 0.0)
            curv = jnp.where(k > 1, d + 2.0 * beta * e + beta * beta * prev[1], d)
            alpha = g / curv
            prev[0] = g
            prev[1] = curv
            prev[2] = alpha
            prev[3] = beta

            def body(row):
                p = UO[row + M4] + beta * Pp[row]
                s = FO[row + W] + beta * S[row]
                Pp[row] = p
                S[row] = s
                x_out[row] = x_out[row] + alpha * p
                r_out[row] = r_out[row] - alpha * s

            loop(own, body, unroll=own)

        @pl.when(k == 0)
        def _():
            prev[2] = jnp.full((cols, 128), -1.0, F32)
            prev[3] = jnp.zeros((cols, 128), F32)

        alpha = prev[2]
        beta = prev[3]
        for m in range(NCB):
            ysm = yw[m] + beta * ys[m]
            ys[m] = ysm
            y[m] = y[m] - alpha * ysm

        solved = jnp.zeros((cols, NCB * 128), F32)
        for m in range(NCB):
            both = halves(y[m])
            part = dot_nn(both, bmat[m * 128 : (m + 1) * 128, :])
            solved = solved + part[0:cols] + part[cols:]
            solved = solved + dot_nn(both[0:cols], bmat2[m * 128 : (m + 1) * 128, :])
        for m in range(NCB):
            zcat[m] = halves(solved[:, m * 128 : (m + 1) * 128])

        def lift(row):
            both = zcat[tab[8, row]]
            part = dot_nn(both, pb[row])
            LVO[row + W] = part[0:cols] + part[cols:] + dot_nn(both[0:cols], pb2[row])

        loop(own, lift, unroll=own)

        @pl.when(k < STAGES - 1)
        def _():
            e = STAGES + k
            pack_send(LVO, LVH, sb.at[e], rb.at[e], exsem_s.at[1 + e], exsem_r.at[1 + e])

        def local_update(i):
            ls = TO[i] + beta * lsO[i]
            lsO[i] = ls
            lO[i] = lO[i] - alpha * ls
            ls = TH[i] + beta * lsH[i]
            lsH[i] = ls
            lH[i] = lH[i] - alpha * ls

        loop(full, local_update, unroll=8)

        @pl.when(k < STAGES - 1)
        def _():
            e = STAGES + k

            def whole(i, o, h):
                UO[i] = o + lO[i]
                UH[i] = h + lH[i]

            assemble(LVO, sb.at[e], rb.at[e], exsem_r.at[1 + e], whole)

            def once(n):
                o, h = apply_row(UO, UH, n + 1)
                AO[n + 1] = o
                AH[n + 1] = h

            loop(full - 2, once, unroll=full - 2)

            def twice(n):
                o, h = apply_row(AO, AH, n + 2)
                FO[n] = o
                FH[n] = near(h)

            loop(ext, twice, unroll=ext)

            def dots(row, acc):
                u = UO[row + M4]
                return (
                    acc[0] + u * r_out[row],
                    acc[1] + u * FO[row + W],
                    acc[2] + u * S[row],
                )

            zero = jnp.zeros((cols, 128), F32)
            dots_send(k + 1, *loop(own, dots, (zero, zero, zero), unroll=own))
            restrict_send(k + 1)

        @pl.when(k == STAGES - 1)
        def _():
            def body(row):
                u_out[row] = lO[row + M4] + LVO[row + W]

            loop(own, body, unroll=own)

        return carry

    lax.fori_loop(0, STAGES, stage, 0)

    pltpu.make_async_copy(irb, irb, exsem_s.at[0]).wait()

    def sent(e):
        pltpu.make_async_copy(rb.at[e], rb.at[e], exsem_s.at[1 + e]).wait()

    loop(2 * STAGES - 1, sent)

    def sent_q(k):
        pltpu.make_async_copy(qar.at[k], qar.at[k], qasem_s.at[k]).wait()
        pltpu.make_async_copy(qbr.at[k], qbr.at[k], qbsem_s.at[k]).wait()

    loop(STAGES, sent_q)

    def sent_d(k):
        pltpu.make_async_copy(dar.at[k + 1], dar.at[k + 1], dasem_s.at[k + 1]).wait()
        pltpu.make_async_copy(dbr.at[k + 1], dbr.at[k + 1], dbsem_s.at[k + 1]).wait()

    loop(STAGES - 1, sent_d)


def sorted_lists(keys, others, count, tiles):
    at = jnp.arange(count, dtype=jnp.int32)
    full_key = keys * 128 + at
    rank = jnp.sum((full_key[None, :] < full_key[:, None]).astype(jnp.int32), axis=1)
    place = rank[None, :] == at[:, None]

    def put(values):
        return jnp.sum(jnp.where(place, values[None, :], 0), axis=1)

    order, partner, key = put(at), put(others), put(keys)
    same = jnp.concatenate([jnp.zeros((1,), jnp.int32), (key[1:] == key[:-1]).astype(jnp.int32)])
    last = jnp.sum((keys[None, :] <= at[:, None]).astype(jnp.int32), axis=1) - 1
    return [order, partner, same, last]


def local(n_b, n_t, right_side, coeff_field, factor_blocks, block_rows, block_cols, prolong, coarse_picks, coarse_factor):
    cols, lat, lon = right_side.shape
    count = factor_blocks.shape[2]
    ext = lat + 2 * W
    full = lat + 2 * M4
    kt = (ext * (lon + 2 * W) + 127) // 128
    nx = 4 if n_t % 4 == 0 and n_t > 4 else 2
    nz = n_t // nx
    rows_idx = block_rows[0, 0]
    cols_idx = block_cols[0, 0]
    picks = jnp.pad(coarse_picks[:, 0, 0], (0, count - lat))
    tab = jnp.stack(
        sorted_lists(rows_idx, cols_idx, count, kt) + sorted_lists(cols_idx, rows_idx, count, kt) + [picks]
    )
    cfg = (n_b, n_t, nx, nz, lat, count, kt, cols)
    n_plane = n_b * nx - 1
    rows24 = cols + 8
    vm = pltpu.VMEM
    ext_f = vm((ext, cols, 128), F32)
    full_f = vm((full, cols, 128), F32)
    own_f = vm((lat, cols, 128), F32)
    n_ex = 2 * STAGES - 1
    dma = pltpu.SemaphoreType.DMA
    scratch = [
        vm((cols, lat, lon), F32),
        vm((lat, lon), F32),
        vm((count, 128, 128), BF16),
        vm((lat, 128, 128), F32),
        vm(coarse_factor.shape[1:], F32),
        vm((lat, 128, 128), BF16),
        vm((lat, 128, 128), BF16),
        vm(coarse_factor.shape[1:], BF16),
        vm(coarse_factor.shape[1:], BF16),
        vm((NCB, 2 * cols, 128), BF16),
        vm((ext, rows24, 128), F32),
        vm((ext, rows24, 128), F32),
        vm((24, rows24, 128), F32),
        vm((24, rows24, 128), F32),
        ext_f,
        ext_f,
        ext_f,
        ext_f,
        vm((n_ex, 24, cols, 128), F32),
        vm((n_ex, 24, cols, 128), F32),
        full_f,
        full_f,
        full_f,
        full_f,
        ext_f,
        ext_f,
        vm((full, 8, 128), F32),
        vm((full, 8, 128), F32),
        full_f,
        full_f,
        full_f,
        full_f,
        full_f,
        full_f,
        own_f,
        own_f,
        vm((NCB, cols, 128), F32),
        vm((NCB, cols, 128), F32),
        vm((NCB, cols, 128), F32),
        vm((kt, cols, 128), BF16),
        vm((kt, cols, 128), BF16),
        vm((count, cols, 128), F32),
        vm((4, cols, 128), F32),
        vm((STAGES, NCB, cols, 128), F32),
        vm((STAGES, nx - 1, NCB, cols, 128), F32),
        vm((STAGES, NCB, cols, 128), BF16),
        vm((STAGES, nz - 1, NCB, cols, 128), BF16),
        vm((STAGES, 8, 128), F32),
        vm((STAGES, n_plane, 8, 128), F32),
        vm((STAGES, 8, 128), F32),
        vm((STAGES, nz - 1, 8, 128), F32),
        dma((5,)),
        dma((1 + n_ex,)),
        dma((1 + n_ex,)),
    ] + [dma((STAGES,))] * 8
    any_spec = pl.BlockSpec(memory_space=pl.ANY)
    out = jax.ShapeDtypeStruct((lat, cols, 128), F32)
    outs = pl.pallas_call(
        functools.partial(kernel, cfg),
        out_shape=(out, out, out),
        in_specs=[pl.BlockSpec(memory_space=pltpu.SMEM)] + [any_spec] * 5,
        out_specs=(pl.BlockSpec(memory_space=pltpu.VMEM),) * 3,
        scratch_shapes=scratch,
        compiler_params=pltpu.CompilerParams(
            collective_id=3, has_side_effects=True, vmem_limit_bytes=48 << 20
        ),
    )(
        tab,
        right_side,
        coeff_field,
        factor_blocks.reshape(factor_blocks.shape[2:]),
        prolong.reshape(lat, 128, lon),
        coarse_factor.reshape(coarse_factor.shape[1:]),
    )
    return tuple(jnp.transpose(value, (1, 0, 2)) for value in outs)


def solution(mesh):
    in_specs = (
        P(None, "band", "tile"),
        P("band", "tile"),
        P("band", "tile", None, None, None),
        P("band", "tile", None),
        P("band", "tile", None),
        P("band", None, None, "tile"),
        P("band", "tile", None),
        P("band", None, None),
    )
    out_specs = (P(None, "band", "tile"),) * 3
    return jax.shard_map(
        functools.partial(local, mesh.shape["band"], mesh.shape["tile"]),
        mesh=mesh,
        in_specs=in_specs,
        out_specs=out_specs,
        check_vma=False,
    )
```

```python
import functools

import jax
import jax.numpy as jnp
from jax import lax
from jax.experimental import pallas as pl
from jax.experimental.pallas import tpu as pltpu
from jax.sharding import PartitionSpec as P

MESH = pl.DeviceIdType.MESH
W = 2
NCB = 4
ITERS = 3
STAGES = ITERS + 1
M4 = 4
F32 = jnp.float32
BF16 = jnp.bfloat16


def loop(count, body, init=None, unroll=1):
    if init is None:

        def step(i, carry):
            body(i)
            return carry

        return lax.fori_loop(0, count, step, 0, unroll=unroll)
    return lax.fori_loop(0, count, body, init, unroll=unroll)


def dot_nn(a, b):
    return lax.dot_general(a, b, (((1,), (0,)), ((), ())), preferred_element_type=F32)


def dot_nt(a, b):
    return lax.dot_general(a, b, (((1,), (1,)), ((), ())), preferred_element_type=F32)


def halves(value):
    high = value.astype(BF16)
    low = (value - high.astype(F32)).astype(BF16)
    return jnp.concatenate([high, low], axis=0)


def kernel(cfg, names, *refs):
    r = dict(zip(names, refs))
    rs_hbm, co_hbm, f_hbm, p_hbm, c_hbm = (r[n] for n in ("rs_hbm", "co_hbm", "f_hbm", "p_hbm", "c_hbm"))
    x_out, r_out = r["xst"], r["rst"]
    picks, tab, tabv, lists = r["picks"], r["tab"], r["tabv"], r["lists"]
    rs, co, fac, pf, cf = r["rs"], r["co"], r["fac"], r["pf"], r["cf"]
    pb, pb2, bmat, bmat2, zcat = r["pb"], r["pb2"], r["bmat"], r["bmat2"], r["zcat"]
    iVO, iVH, isb, irb = r["iVO"], r["iVH"], r["isb"], r["irb"]
    VO, VH, sb, rb = r["VO"], r["VH"], r["sb"], r["rb"]
    LV, pk, nsb, nrb = r["LV"], r["pk"], r["nsb"], r["nrb"]
    pht, phr, ph, ph2, pm = r["pht"], r["phr"], r["ph"], r["ph2"], r["pm"]
    UO, UH, AO, AH, FO, FH = r["UO"], r["UH"], r["AO"], r["AH"], r["FO"], r["FH"]
    c4O, c4H, MsO, MsH, TO, TH = r["c4O"], r["c4H"], r["MsO"], r["MsH"], r["TO"], r["TH"]
    S, Pp, yw, xin, gin, run, prev = r["S"], r["Pp"], r["yw"], r["xin"], r["gin"], r["run"], r["prev"]
    qa, qar, qb, qbr = r["qa"], r["qar"], r["qb"], r["qbr"]
    da, dar, db, dbr = r["da"], r["dar"], r["db"], r["dbr"]
    insem, exsem_s, exsem_r = r["insem"], r["exsem_s"], r["exsem_r"]
    nssem_s, nssem_r, phsem_s, phsem_r = r["nssem_s"], r["nssem_r"], r["phsem_s"], r["phsem_r"]
    qasem_s, qasem_r, qbsem_s, qbsem_r = r["qasem_s"], r["qasem_r"], r["qbsem_s"], r["qbsem_r"]
    dasem_s, dasem_r, dbsem_s, dbsem_r = r["dasem_s"], r["dasem_r"], r["dbsem_s"], r["dbsem_r"]
    n_b, n_t, nx, nz, lat, nb_blocks, kt, cols = cfg
    b = lax.axis_index("band")
    t = lax.axis_index("tile")
    z = t // nx
    x = t % nx
    own = lat
    ext = lat + 2 * W
    full = lat + 2 * M4

    sources = (r["br_hbm"], r["bc_hbm"], rs_hbm, co_hbm, p_hbm, c_hbm, f_hbm)
    targets = (r["br"], r["bc"], rs, co, pf, cf, fac)
    loads = [pltpu.make_async_copy(a, c, insem.at[n]) for n, (a, c) in enumerate(zip(sources, targets))]
    for copy in loads:
        copy.start()

    def band_at(d):
        return lax.rem(b + d + n_b, n_b)

    def tile_at(d):
        return lax.rem(t + d + n_t, n_t)

    def x_peer(d):
        return (b, z * nx + lax.rem(x + d, nx))

    def z_peer(d):
        return (b, lax.rem(t + nx * d, n_t))

    def plane_peer(d):
        return (lax.rem(b + d // nx, n_b), z * nx + lax.rem(x + lax.rem(d, nx), nx))

    n_plane = n_b * nx - 1
    barrier = pltpu.get_barrier_semaphore()

    def greet(device):
        pl.semaphore_signal(barrier, inc=1, device_id=device, device_id_type=MESH)

    loop(n_plane, lambda d: greet(plane_peer(d + 1)))
    loop(nz - 1, lambda d: greet(z_peer(d + 1)))
    for db_ in (-1, 0, 1):
        for dt_ in (-1, 1):
            greet((band_at(db_), tile_at(dt_)))

    has_n = (b > 0).astype(F32)
    has_s = (b < n_b - 1).astype(F32)
    has_w = (t > 0).astype(F32)
    has_e = (t < n_t - 1).astype(F32)

    def lane_of(rows):
        return lax.broadcasted_iota(jnp.int32, (rows, 128), 1)

    def pack(vO, vH, sbe):
        rows = vO.shape[1]
        lane = lane_of(rows)
        west_half = lane >= 64
        group = lane // 8
        zero = jnp.zeros((rows, 128), F32)

        def half(first_slot, first_row):
            def body(n, carry):
                tw, te = carry
                slot = first_slot + n
                row = first_row + n
                o = vO[row]
                h = vH[row]
                shift = lax.rem(8 * slot + 4, 128)
                here = group == slot
                w = pltpu.roll(jnp.where(west_half, h, o), shift, 1)
                e = pltpu.roll(jnp.where(west_half, o, h), shift, 1)
                return tw + jnp.where(here, w, 0.0), te + jnp.where(here, e, 0.0)

            return loop(ext // 2, body, (zero, zero), unroll=ext // 2)

        tw0, te0 = half(2, 0)
        tw1, te1 = half(0, ext // 2)
        for n in range(6):
            sbe[n] = vO[n]
            sbe[8 + n] = vO[ext - 6 + n]
        sbe[6] = tw0
        sbe[7] = te0
        sbe[14] = tw1
        sbe[15] = te1
        sbe[16] = te0
        sbe[17] = te1
        sbe[18] = tw0
        sbe[19] = tw1

    def send_eight(sbe, rbe, ssem, rsem):
        for first, count, to, db_, dt_ in (
            (0, 8, 8, -1, 0),
            (8, 8, 0, 1, 0),
            (16, 2, 18, 0, 1),
            (18, 2, 16, 0, -1),
            (16, 1, 22, -1, 1),
            (17, 1, 20, 1, 1),
            (18, 1, 23, -1, -1),
            (19, 1, 21, 1, -1),
        ):
            pltpu.make_async_remote_copy(
                src_ref=sbe.at[pl.ds(first, count)],
                dst_ref=rbe.at[pl.ds(to, count)],
                send_sem=ssem,
                recv_sem=rsem,
                device_id=(band_at(db_), tile_at(dt_)),
                device_id_type=MESH,
            ).start()

    def assemble(vO, sbe, rbe, rsem, emit):
        rows = vO.shape[1]
        lane = lane_of(rows)
        pltpu.make_async_copy(rbe, rbe, rsem).wait()
        low = jnp.where(lane < 48, 1.0, 0.0)
        high = jnp.where(lane >= 80, 1.0, 0.0)
        m_w = jnp.where(lane >= 124, has_w, 0.0)
        m_e = jnp.where(lane < 4, has_e, 0.0)

        def turned(slot):
            return pltpu.roll(rbe[slot], 64, 1)

        pw = (
            sbe[18] + has_w * rbe[18] + (has_n * low) * (turned(6) + has_w * turned(20)),
            sbe[19] + has_w * rbe[19] + (has_s * high) * (turned(14) + has_w * turned(22)),
        )
        pe = (
            sbe[16] + has_e * rbe[16] + (has_n * low) * (turned(7) + has_e * turned(21)),
            sbe[17] + has_e * rbe[17] + (has_s * high) * (turned(15) + has_e * turned(23)),
        )

        def finish(o, slot, half, scale, i):
            shift = lax.rem(124 - 8 * slot + 128, 128)
            w = pltpu.roll(pw[half], shift, 1)
            e = pltpu.roll(pe[half], shift, 1)
            o = jnp.where(lane < 4, w, jnp.where(lane >= 124, e, o))
            h = w * m_w + e * m_e
            if scale is not None:
                o = o * scale
                h = h * scale
            emit(i, o, h)

        for i in range(6):
            o = has_n * rbe[i]
            if i >= 2:
                o = o + vO[i - 2]
            finish(o, i, 0, has_n if i < M4 else None, i)
        mid0 = 10
        mid1 = full - 6 - 16

        def body0(n):
            finish(vO[4 + n], 6 + n, 0, None, 6 + n)

        def body1(n):
            finish(vO[14 + n], n, 1, None, 16 + n)

        loop(mid0, body0, unroll=mid0)
        loop(mid1, body1, unroll=mid1)
        for n in range(6):
            i = full - 6 + n
            o = has_s * rbe[8 + n]
            if i < full - 2:
                o = o + vO[i - 2]
            finish(o, i - 16, 1, has_s if i >= full - M4 else None, i)

    def restrict(first, count, acc):
        def body(n, acc):
            row = first + n
            both = halves(FO[row + W])
            part = dot_nt(both, pb[row])
            part = part[0:cols] + part[cols:] + dot_nt(both[0:cols], pb2[row])
            pick = picks[row]
            return tuple(acc[m] + part * (pick == m).astype(F32) for m in range(NCB))

        return loop(count, body, acc, unroll=count)

    def send_x(k):
        for d in range(nx - 1):
            pltpu.make_async_remote_copy(
                src_ref=qa.at[k],
                dst_ref=qar.at[k, d],
                send_sem=qasem_s.at[k],
                recv_sem=qasem_r.at[k],
                device_id=x_peer(d + 1),
                device_id_type=MESH,
            ).start()

    def dots_send(k, gamma, delta, eps):
        lane = lane_of(cols)
        g = jnp.sum(gamma, axis=1, keepdims=True)
        d = jnp.sum(delta, axis=1, keepdims=True)
        e = jnp.sum(eps, axis=1, keepdims=True)
        tile = (
            jnp.where(lane == 0, g, 0.0) + jnp.where(lane == 1, d, 0.0) + jnp.where(lane == 2, e, 0.0)
        )
        da[k] = tile[0:8] + pltpu.roll(tile[8:16], 64, 1)

        def send(d):
            pltpu.make_async_remote_copy(
                src_ref=da.at[k],
                dst_ref=dar.at[k, d],
                send_sem=dasem_s.at[k],
                recv_sem=dasem_r.at[k],
                device_id=plane_peer(d + 1),
                device_id_type=MESH,
            ).start()

        loop(n_plane, send)

    def reduce_mid(k):
        pltpu.make_async_copy(qar.at[k], qar.at[k], qasem_r.at[k]).wait()
        for m in range(NCB):
            total = qa[k, m]
            for d in range(nx - 1):
                total = total + qar[k, d, m]
            qb[k, m] = total.astype(BF16)

        def send_q(d):
            pltpu.make_async_remote_copy(
                src_ref=qb.at[k],
                dst_ref=qbr.at[k, d],
                send_sem=qbsem_s.at[k],
                recv_sem=qbsem_r.at[k],
                device_id=z_peer(d + 1),
                device_id_type=MESH,
            ).start()

        for d in range(nz - 1):
            send_q(d)

    def dots_mid(k):
        pltpu.make_async_copy(dar.at[k], dar.at[k], dasem_r.at[k]).wait()
        total = da[k]
        for d in range(n_plane):
            total = total + dar[k, d]
        db[k] = total

        def send_d(d):
            pltpu.make_async_remote_copy(
                src_ref=db.at[k],
                dst_ref=dbr.at[k, d],
                send_sem=dbsem_s.at[k],
                recv_sem=dbsem_r.at[k],
                device_id=z_peer(d + 1),
                device_id_type=MESH,
            ).start()

        for d in range(nz - 1):
            send_d(d)

    def reduce_end(k):
        pltpu.make_async_copy(qbr.at[k], qbr.at[k], qbsem_r.at[k]).wait()
        for m in range(NCB):
            total = qb[k, m].astype(F32)
            for d in range(nz - 1):
                total = total + qbr[k, d, m].astype(F32)
            yw[m] = total

    def dots_end(k):
        pltpu.make_async_copy(dbr.at[k], dbr.at[k], dbsem_r.at[k]).wait()
        total = db[k]
        for d in range(nz - 1):
            total = total + dbr[k, d]
        tile = jnp.concatenate([total, pltpu.roll(total, 64, 1)], axis=0)
        shape = (cols, 128)
        return tuple(jnp.broadcast_to(tile[:, n : n + 1], shape) for n in range(3))

    def local_solve():
        lane = lane_of(cols)
        zero = jnp.zeros((cols, 128), F32)

        def flatten(j, carry):
            s = 4 * j + W
            o = pltpu.roll(FO[j], s, 1)
            h = pltpu.roll(FH[j], s, 1)
            late = lane >= s
            xin[j] = (jnp.where(late, o, h) + carry).astype(BF16)
            return jnp.where(late, h, o)

        tail = loop(ext, flatten, zero, unroll=ext)
        xin[ext] = tail.astype(BF16)

        def inner(n, acc):
            acc = acc * tab[2, n].astype(F32) + dot_nt(xin[tab[1, n]], fac[tab[0, n]])
            run[n] = acc
            return acc

        loop(nb_blocks, inner, zero, unroll=nb_blocks)

        def gather(i):
            gin[i] = run[tab[3, i]].astype(BF16)

        loop(kt, gather, unroll=kt)

        def outer(n, acc):
            acc = acc * tab[6, n].astype(F32) + dot_nn(gin[tab[5, n]], fac[tab[4, n]])
            run[n] = acc
            return acc

        loop(nb_blocks, outer, zero, unroll=nb_blocks)

        def unflatten(j, carry):
            s = 4 * j + W
            following = run[tab[7, j + 1]]
            here = pltpu.roll(carry, 128 - s, 1)
            there = pltpu.roll(following, 128 - s, 1)
            VO[j] = jnp.where(lane < 128 - s, here, there)
            VH[j] = jnp.where(lane >= 126, here, jnp.where(lane < 2, there, 0.0))
            return following

        loop(ext, unflatten, run[tab[7, 0]], unroll=ext)

    def near(value):
        lane = lane_of(cols)
        return jnp.where((lane < W) | (lane >= 128 - W), value, 0.0)

    def spread_out(row):
        return jnp.broadcast_to(row, (128, 128))

    lane128 = lane_of(128)
    sub128 = lax.broadcasted_iota(jnp.int32, (128, 128), 0)

    def sort_list(first, keys, others):
        keys_sub = jnp.transpose(spread_out(keys))
        others_sub = jnp.transpose(spread_out(others))
        key_lane = spread_out(keys) * 128 + lane128
        key_sub = keys_sub * 128 + sub128
        rank = jnp.sum((key_lane < key_sub).astype(jnp.int32), axis=1, keepdims=True)
        place = rank == lane128

        def put(values):
            return jnp.sum(jnp.where(place, values, 0), axis=0, keepdims=True)

        ordered = put(keys_sub)
        before = pltpu.roll(ordered, 1, 1)
        same = jnp.where((ordered == before) & (lane128[0:1] > 0), 1, 0)
        tabv[first : first + 1, :] = put(sub128)
        tabv[first + 1 : first + 2, :] = put(others_sub)
        tabv[first + 2 : first + 3, :] = same
        tabv[first + 3 : first + 4, :] = (
            jnp.sum((keys_sub <= lane128).astype(jnp.int32), axis=0, keepdims=True) - 1
        )

    lists[...] = jnp.full(lists.shape, 100, jnp.int32)
    loads[0].wait()
    loads[1].wait()
    lists[0:1, 0:nb_blocks] = r["br"][0]
    lists[1:2, 0:nb_blocks] = r["bc"][0]
    sort_list(0, lists[0:1, :], lists[1:2, :])
    sort_list(4, lists[1:2, :], lists[0:1, :])
    to_smem = pltpu.make_async_copy(tabv, tab, insem.at[7])
    to_smem.start()

    rows24 = cols + 8
    zero24 = jnp.zeros((rows24, 128), F32)
    zero = jnp.zeros((cols, 128), F32)
    lane16 = lane_of(cols)
    for row in (0, 1, ext - 2, ext - 1):
        iVO[row] = zero24
    iVH[...] = jnp.zeros(iVH.shape, F32)
    for ref in (UO, UH, MsO, MsH, S, Pp):
        ref[...] = jnp.zeros(ref.shape, F32)
    prev[...] = jnp.ones(prev.shape, F32)
    prev[2] = jnp.full((cols, 128), -1.0, F32)
    prev[3] = zero

    loads[2].wait()
    loads[3].wait()
    for row in range(own):
        value = rs[:, row, :]
        r_out[row] = value
        FO[row + W] = value
        x_out[row] = zero
        iVO[W + row, 0:cols] = value
        iVO[W + row, cols:rows24] = jnp.broadcast_to(co[row : row + 1, :], (8, 128))
    pack(iVO, iVH, isb)

    loads[4].wait()

    def to_bf16(row):
        value = pf[row]
        high = value.astype(BF16)
        pb[row] = high
        pb2[row] = (value - high.astype(F32)).astype(BF16)

    loop(own, to_bf16, unroll=4)
    acc = restrict(0, own, (zero,) * NCB)
    for m in range(NCB):
        qa[0, m] = acc[m]

    group128 = lane128 // 8
    group8 = group128[0:8]
    sub8 = sub128[0:8]
    for half, first_slot, first_row in ((0, M4, 0), (1, 0, 16 - M4)):

        def columns(n, carry):
            slot = first_slot + n
            turned = pltpu.roll(pf[first_row + n], lax.rem(8 * slot + 4, 128), 1)
            chosen = (group8 == slot) & (sub8 == picks[first_row + n])
            return (
                carry[0] + jnp.where(group128 == slot, turned, 0.0),
                carry[1] + jnp.where(chosen, 1.0, 0.0),
            )

        values, masks = loop(
            own // 2, columns, (jnp.zeros((128, 128), F32), jnp.zeros((8, 128), F32)), unroll=4
        )
        pht[half, 0:128] = values
        pht[half, 128:136] = masks

    pl.semaphore_wait(barrier, n_plane + nz - 1 + 6)
    send_eight(isb, irb, exsem_s.at[0], exsem_r.at[0])
    send_x(0)
    for n, d in enumerate((1, -1)):
        pltpu.make_async_remote_copy(
            src_ref=pht,
            dst_ref=phr.at[n],
            send_sem=phsem_s.at[n],
            recv_sem=phsem_r.at[n],
            device_id=(b, tile_at(d)),
            device_id_type=MESH,
        ).start()

    loads[5].wait()
    for m in range(NCB):
        value = lax.dot_general(
            cf[:, m * 128 : (m + 1) * 128],
            cf[...],
            (((0,), (0,)), ((), ())),
            precision=lax.Precision.HIGHEST,
            preferred_element_type=F32,
        )
        high = value.astype(BF16)
        bmat[m * 128 : (m + 1) * 128, :] = high
        bmat2[m * 128 : (m + 1) * 128, :] = (value - high.astype(F32)).astype(BF16)

    def take_first(i, o, h):
        if isinstance(i, int):
            keep = W <= i < full - W
        else:
            keep = True
        if keep:
            FO[i - W] = o[0:cols]
            FH[i - W] = near(h[0:cols])
        inside = 0.25
        if isinstance(i, int):
            if i < M4:
                inside = 0.25 * has_n
            elif i >= full - M4:
                inside = 0.25 * has_s
        lane8 = lane16[0:8]
        side = jnp.where(lane8 >= 128 - M4, has_w, 0.0) + jnp.where(lane8 < M4, has_e, 0.0)
        c4O[i] = (o[cols:rows24] + 4.0) * inside
        c4H[i] = (h[cols:rows24] + 4.0) * (side * inside)

    assemble(iVO, isb, irb, exsem_r.at[0], take_first)
    loads[6].wait()
    to_smem.wait()

    side16 = jnp.where(lane16 >= 128 - M4, has_w, 0.0) + jnp.where(lane16 < M4, has_e, 0.0)
    last_lane = lane16 == 127
    first_lane = lane16 == 0

    def row_scale(i):
        north = jnp.where(i < M4, has_n, 1.0)
        south = jnp.where(i >= full - M4, has_s, 1.0)
        return 0.25 * north * south

    def apply_row(srcO, srcH, i):
        o = srcO[i]
        h = srcH[i]
        ol = pltpu.roll(o, 1, 1)
        hl = pltpu.roll(h, 1, 1)
        orr = pltpu.roll(o, 127, 1)
        hr = pltpu.roll(h, 127, 1)
        around_o = (
            srcO[i - 1]
            + srcO[i + 1]
            + jnp.where(first_lane, hl, ol)
            + jnp.where(last_lane, hr, orr)
        )
        around_h = (
            srcH[i - 1]
            + srcH[i + 1]
            + jnp.where(first_lane, ol, hl)
            + jnp.where(last_lane, orr, hr)
        )
        scale = row_scale(i)
        co_ = jnp.concatenate([c4O[i], c4O[i]], axis=0)
        ch_ = jnp.concatenate([c4H[i], c4H[i]], axis=0)
        return co_ * o - scale * around_o, ch_ * h - (scale * side16) * around_h

    def once(i):
        o, h = apply_row(UO, UH, i)
        AO[i] = o
        AH[i] = h

    def twice(i):
        o, h = apply_row(AO, AH, i)
        FO[i - W] = o
        FH[i - W] = near(h)

    def lift(first, count):
        def body(n):
            row = first + n
            both = zcat[picks[row]]
            part = dot_nn(both, pb[row])
            LV[row] = part[0:cols] + part[cols:] + dot_nn(both[0:cols], pb2[row])

        loop(count, body, unroll=count)

    def stage(k, carry):
        local_solve()
        reduce_mid(k)
        pack(VO, VH, sb.at[k])
        send_eight(sb.at[k], rb.at[k], exsem_s.at[1 + k], exsem_r.at[1 + k])

        @pl.when(k > 0)
        def _():
            dots_mid(k)

        @pl.when(k == 0)
        def _():
            for n in range(2):
                pltpu.make_async_copy(phr.at[n], phr.at[n], phsem_r.at[n]).wait()
            from_west = lax.rem(lane128, 8) < M4
            for half in range(2):
                value = jnp.where(from_west, has_w * phr[0, half, 0:128], has_e * phr[1, half, 0:128])
                high = value.astype(BF16)
                ph[half] = high
                ph2[half] = (value - high.astype(F32)).astype(BF16)
                pm[half] = jnp.where(from_west[0:8], phr[0, half, 128:136], phr[1, half, 128:136])

        def keep(i, o, h):
            TO[i] = o
            TH[i] = h

        assemble(VO, sb.at[k], rb.at[k], exsem_r.at[1 + k], keep)
        reduce_end(k)

        solved = jnp.zeros((cols, NCB * 128), F32)
        for m in range(NCB):
            both = halves(yw[m])
            part = dot_nn(both, bmat[m * 128 : (m + 1) * 128, :])
            solved = solved + part[0:cols] + part[cols:]
            solved = solved + dot_nn(both[0:cols], bmat2[m * 128 : (m + 1) * 128, :])
        for m in range(NCB):
            zcat[m] = halves(solved[:, m * 128 : (m + 1) * 128])
        lift(0, M4)
        lift(own - M4, M4)
        for half in range(2):
            total = zero
            for m in range(NCB):
                both = zcat[m]
                part = dot_nn(both, ph[half])
                part = part[0:cols] + part[cols:] + dot_nn(both[0:cols], ph2[half])
                total = total + part * jnp.broadcast_to(pm[half, m : m + 1, :], (cols, 128))
            pk[half] = total

        @pl.when(k < STAGES - 1)
        def _():
            for n in range(M4):
                nsb[k, n] = LV[n]
                nsb[k, M4 + 1 + n] = LV[own - M4 + n]
            nsb[k, M4] = pk[0]
            nsb[k, 2 * M4 + 1] = pk[1]
            for first, to, d in ((0, M4 + 1, -1), (M4 + 1, 0, 1)):
                pltpu.make_async_remote_copy(
                    src_ref=nsb.at[k, pl.ds(first, M4 + 1)],
                    dst_ref=nrb.at[k, pl.ds(to, M4 + 1)],
                    send_sem=nssem_s.at[k],
                    recv_sem=nssem_r.at[k],
                    device_id=(band_at(d), t),
                    device_id_type=MESH,
                ).start()

        lift(M4, own - 2 * M4)

        @pl.when(k > 0)
        def _():
            g, d, e = dots_end(k)
            beta = jnp.where(k > 1, g / prev[0], 0.0)
            curv = jnp.where(k > 1, d + 2.0 * beta * e + beta * beta * prev[1], d)
            alpha = g / curv
            prev[0] = g
            prev[1] = curv
            prev[2] = alpha
            prev[3] = beta

            def body(row):
                p = UO[row + M4] + beta * Pp[row]
                s = FO[row + W] + beta * S[row]
                Pp[row] = p
                S[row] = s
                x_out[row] = x_out[row] + alpha * p
                r_out[row] = r_out[row] - alpha * s

            loop(own, body, unroll=own)

        alpha = prev[2]
        beta = prev[3]

        def combine(i, o, h):
            ms = TO[i] + o + beta * MsO[i]
            MsO[i] = ms
            UO[i] = UO[i] - alpha * ms
            ms = TH[i] + h + beta * MsH[i]
            MsH[i] = ms
            UH[i] = UH[i] - alpha * ms

        for half, first_slot, first_row in ((0, M4, 0), (1, 0, 16 - M4)):
            strip = pk[half]

            def inner_rows(n):
                slot = first_slot + n
                h = pltpu.roll(strip, lax.rem(252 - 8 * slot, 128), 1) * side16
                combine(16 * half + slot, LV[first_row + n], h)

            loop(own // 2, inner_rows, unroll=own // 2)

        @pl.when(k < STAGES - 1)
        def _():
            loop(full - 10, lambda n: once(5 + n), unroll=full - 10)
            loop(full - 12, lambda n: twice(6 + n), unroll=full - 12)
            acc = restrict(2, own - 4, (zero,) * NCB)

            pltpu.make_async_copy(nrb.at[k], nrb.at[k], nssem_r.at[k]).wait()
            for n in range(M4):
                combine(n, nrb[k, n] * has_n, pltpu.roll(nrb[k, M4], 60 - 8 * n, 1) * (has_n * side16))
                combine(
                    full - M4 + n,
                    nrb[k, M4 + 1 + n] * has_s,
                    pltpu.roll(nrb[k, 2 * M4 + 1], 92 - 8 * n, 1) * (has_s * side16),
                )
            for n in range(4):
                once(1 + n)
                once(full - 5 + n)
            for n in range(4):
                twice(2 + n)
                twice(full - 6 + n)
            acc = restrict(0, 2, acc)
            acc = restrict(own - 2, 2, acc)
            for m in range(NCB):
                qa[k + 1, m] = acc[m]
            send_x(k + 1)

            def dots(row, acc):
                u = UO[row + M4]
                return (
                    acc[0] + u * r_out[row],
                    acc[1] + u * FO[row + W],
                    acc[2] + u * S[row],
                )

            dots_send(k + 1, *loop(own, dots, (zero, zero, zero), unroll=own))

        @pl.when(k == STAGES - 1)
        def _():
            def body(row):
                r["x_out"][:, row, :] = x_out[row]
                r["r_out"][:, row, :] = r_out[row]
                r["u_out"][:, row, :] = UO[row + M4]

            loop(own, body, unroll=own)

        return carry

    lax.fori_loop(0, STAGES, stage, 0)

    pltpu.make_async_copy(irb, irb, exsem_s.at[0]).wait()

    def sent(e):
        pltpu.make_async_copy(rb.at[e], rb.at[e], exsem_s.at[1 + e]).wait()

    loop(STAGES, sent)
    for n in range(2):
        pltpu.make_async_copy(phr.at[n], phr.at[n], phsem_s.at[n]).wait()

    def sent_ns(k):
        pltpu.make_async_copy(nrb.at[k], nrb.at[k], nssem_s.at[k]).wait()

    loop(STAGES - 1, sent_ns)

    def sent_q(k):
        pltpu.make_async_copy(qar.at[k], qar.at[k], qasem_s.at[k]).wait()
        pltpu.make_async_copy(qbr.at[k], qbr.at[k], qbsem_s.at[k]).wait()

    loop(STAGES, sent_q)

    def sent_d(k):
        pltpu.make_async_copy(dar.at[k + 1], dar.at[k + 1], dasem_s.at[k + 1]).wait()
        pltpu.make_async_copy(dbr.at[k + 1], dbr.at[k + 1], dbsem_s.at[k + 1]).wait()

    loop(STAGES - 1, sent_d)


def local(n_b, n_t, right_side, coeff_field, factor_blocks, block_rows, block_cols, prolong, coarse_picks, coarse_factor):
    cols, lat, lon = right_side.shape
    count = factor_blocks.shape[2]
    ext = lat + 2 * W
    full = lat + 2 * M4
    kt = (ext * (lon + 2 * W) + 127) // 128
    nx = 4 if n_t % 4 == 0 and n_t > 4 else 2
    nz = n_t // nx
    cfg = (n_b, n_t, nx, nz, lat, count, kt, cols)
    n_plane = n_b * nx - 1
    rows24 = cols + 8
    vm = pltpu.VMEM
    ext_f = vm((ext, cols, 128), F32)
    full_f = vm((full, cols, 128), F32)
    own_f = vm((lat, cols, 128), F32)
    cn = coarse_factor.shape[1:]
    four = vm((NCB, cols, 128), F32)
    dma = pltpu.SemaphoreType.DMA
    scratch = dict(
        tab=pltpu.SMEM((8, 128), jnp.int32),
        tabv=vm((8, 128), jnp.int32),
        lists=vm((8, 128), jnp.int32),
        br=vm((1, 1, count), jnp.int32),
        bc=vm((1, 1, count), jnp.int32),
        rs=vm((cols, lat, lon), F32),
        co=vm((lat, lon), F32),
        fac=vm((count, 128, 128), BF16),
        pf=vm((lat, 128, 128), F32),
        cf=vm(cn, F32),
        pb=vm((lat, 128, 128), BF16),
        pb2=vm((lat, 128, 128), BF16),
        bmat=vm(cn, BF16),
        bmat2=vm(cn, BF16),
        zcat=vm((NCB, 2 * cols, 128), BF16),
        iVO=vm((ext, rows24, 128), F32),
        iVH=vm((ext, rows24, 128), F32),
        isb=vm((24, rows24, 128), F32),
        irb=vm((24, rows24, 128), F32),
        VO=ext_f,
        VH=ext_f,
        sb=vm((STAGES, 24, cols, 128), F32),
        rb=vm((STAGES, 24, cols, 128), F32),
        LV=own_f,
        pk=vm((2, cols, 128), F32),
        nsb=vm((ITERS, 2 * M4 + 2, cols, 128), F32),
        nrb=vm((ITERS, 2 * M4 + 2, cols, 128), F32),
        pht=vm((2, 136, 128), F32),
        phr=vm((2, 2, 136, 128), F32),
        ph=vm((2, 128, 128), BF16),
        ph2=vm((2, 128, 128), BF16),
        pm=vm((2, 8, 128), F32),
        UO=full_f,
        UH=full_f,
        AO=full_f,
        AH=full_f,
        FO=ext_f,
        FH=ext_f,
        c4O=vm((full, 8, 128), F32),
        c4H=vm((full, 8, 128), F32),
        MsO=full_f,
        MsH=full_f,
        TO=full_f,
        TH=full_f,
        xst=own_f,
        rst=own_f,
        S=own_f,
        Pp=own_f,
        yw=four,
        xin=vm((kt, cols, 128), BF16),
        gin=vm((kt, cols, 128), BF16),
        run=vm((count, cols, 128), F32),
        prev=vm((4, cols, 128), F32),
        qa=vm((STAGES, NCB, cols, 128), F32),
        qar=vm((STAGES, nx - 1, NCB, cols, 128), F32),
        qb=vm((STAGES, NCB, cols, 128), BF16),
        qbr=vm((STAGES, nz - 1, NCB, cols, 128), BF16),
        da=vm((STAGES, 8, 128), F32),
        dar=vm((STAGES, n_plane, 8, 128), F32),
        db=vm((STAGES, 8, 128), F32),
        dbr=vm((STAGES, nz - 1, 8, 128), F32),
        insem=dma((8,)),
        exsem_s=dma((1 + STAGES,)),
        exsem_r=dma((1 + STAGES,)),
        nssem_s=dma((ITERS,)),
        nssem_r=dma((ITERS,)),
        phsem_s=dma((2,)),
        phsem_r=dma((2,)),
    )
    for name in ("qasem_s", "qasem_r", "qbsem_s", "qbsem_r", "dasem_s", "dasem_r", "dbsem_s", "dbsem_r"):
        scratch[name] = dma((STAGES,))
    inputs = dict(
        picks=coarse_picks.reshape(lat),
        br_hbm=block_rows.reshape(1, 1, count),
        bc_hbm=block_cols.reshape(1, 1, count),
        rs_hbm=right_side,
        co_hbm=coeff_field,
        f_hbm=factor_blocks.reshape(factor_blocks.shape[2:]),
        p_hbm=prolong.reshape(lat, 128, lon),
        c_hbm=coarse_factor.reshape(cn),
    )
    results = ("x_out", "r_out", "u_out")
    out = jax.ShapeDtypeStruct((cols, lat, 128), F32)
    outs = pl.pallas_call(
        functools.partial(kernel, cfg, tuple(inputs) + results + tuple(scratch)),
        out_shape=(out, out, out),
        in_specs=[pl.BlockSpec(memory_space=pltpu.SMEM)]
        + [pl.BlockSpec(memory_space=pltpu.HBM)] * (len(inputs) - 1),
        out_specs=(pl.BlockSpec(memory_space=pltpu.VMEM),) * 3,
        scratch_shapes=list(scratch.values()),
        compiler_params=pltpu.CompilerParams(
            collective_id=3, has_side_effects=True, vmem_limit_bytes=63 << 20
        ),
    )(*inputs.values())

    def hand_on(*refs):
        for n in range(3):
            refs[3 + n][...] = refs[n][...]

    return pl.pallas_call(
        hand_on,
        out_shape=(out, out, out),
    )(*outs)


def solution(mesh):
    in_specs = (
        P(None, "band", "tile"),
        P("band", "tile"),
        P("band", "tile", None, None, None),
        P("band", "tile", None),
        P("band", "tile", None),
        P("band", None, None, "tile"),
        P("band", "tile", None),
        P("band", None, None),
    )
    out_specs = (P(None, "band", "tile"),) * 3
    return jax.shard_map(
        functools.partial(local, mesh.shape["band"], mesh.shape["tile"]),
        mesh=mesh,
        in_specs=in_specs,
        out_specs=out_specs,
        check_vma=False,
    )
```

```python
import functools

import jax
import jax.numpy as jnp
from jax import lax
from jax.experimental import pallas as pl
from jax.experimental.pallas import tpu as pltpu
from jax.sharding import PartitionSpec as P

MESH = pl.DeviceIdType.MESH
W = 2
NCB = 4
ITERS = 3
STAGES = ITERS + 1
M4 = 4
F32 = jnp.float32
BF16 = jnp.bfloat16


def loop(count, body, init=None, unroll=1):
    if init is None:

        def step(i, carry):
            body(i)
            return carry

        return lax.fori_loop(0, count, step, 0, unroll=unroll)
    return lax.fori_loop(0, count, body, init, unroll=unroll)


def dot_nn(a, b):
    return lax.dot_general(a, b, (((1,), (0,)), ((), ())), preferred_element_type=F32)


def dot_nt(a, b):
    return lax.dot_general(a, b, (((1,), (1,)), ((), ())), preferred_element_type=F32)


def far_first(count):
    return sorted(range(1, count), key=lambda d: -min(d, count - d))


def halves(value):
    high = value.astype(BF16)
    low = (value - high.astype(F32)).astype(BF16)
    return jnp.concatenate([high, low], axis=0)


def kernel(cfg, names, *refs):
    r = dict(zip(names, refs))
    rs_hbm, co_hbm, f_hbm, p_hbm, c_hbm = (r[n] for n in ("rs_hbm", "co_hbm", "f_hbm", "p_hbm", "c_hbm"))
    x_out, r_out = r["xst"], r["rst"]
    picks, tab, tabv, lists = r["picks"], r["tab"], r["tabv"], r["lists"]
    rs, co, fac, pf, cf = r["rs"], r["co"], r["fac"], r["pf"], r["cf"]
    pb, pb2, bmat, bmat2, zcat = r["pb"], r["pb2"], r["bmat"], r["bmat2"], r["zcat"]
    iVO, iVH, isb, irb = r["iVO"], r["iVH"], r["isb"], r["irb"]
    VO, VH, sb, rb = r["VO"], r["VH"], r["sb"], r["rb"]
    LV, pk, nsb, nrb = r["LV"], r["pk"], r["nsb"], r["nrb"]
    pht, phr, ph, ph2, pm = r["pht"], r["phr"], r["ph"], r["ph2"], r["pm"]
    UO, UH, AO, AH, FO, FH = r["UO"], r["UH"], r["AO"], r["AH"], r["FO"], r["FH"]
    c4O, c4H, MsO, MsH, TO, TH = r["c4O"], r["c4H"], r["MsO"], r["MsH"], r["TO"], r["TH"]
    S, Pp, yw, xin, gin, run, prev = r["S"], r["Pp"], r["yw"], r["xin"], r["gin"], r["run"], r["prev"]
    qa, qar, qb, qbr = r["qa"], r["qar"], r["qb"], r["qbr"]
    da, dar, db, dbr = r["da"], r["dar"], r["db"], r["dbr"]
    insem, exsem_s, exsem_r = r["insem"], r["exsem_s"], r["exsem_r"]
    nssem_s, nssem_r, phsem_s, phsem_r = r["nssem_s"], r["nssem_r"], r["phsem_s"], r["phsem_r"]
    qasem_s, qasem_r, qbsem_s, qbsem_r = r["qasem_s"], r["qasem_r"], r["qbsem_s"], r["qbsem_r"]
    dasem_s, dasem_r, dbsem_s, dbsem_r = r["dasem_s"], r["dasem_r"], r["dbsem_s"], r["dbsem_r"]
    n_b, n_t, nx, nz, lat, nb_blocks, kt, cols = cfg
    b = lax.axis_index("band")
    t = lax.axis_index("tile")
    z = t // nx
    x = t % nx
    own = lat
    ext = lat + 2 * W
    full = lat + 2 * M4

    sources = (r["br_hbm"], r["bc_hbm"], rs_hbm, co_hbm, p_hbm, c_hbm, f_hbm)
    targets = (r["br"], r["bc"], rs, co, pf, cf, fac)
    loads = [pltpu.make_async_copy(a, c, insem.at[n]) for n, (a, c) in enumerate(zip(sources, targets))]
    for copy in loads:
        copy.start()

    def band_at(d):
        return lax.rem(b + d + n_b, n_b)

    def tile_at(d):
        return lax.rem(t + d + n_t, n_t)

    def x_peer(d):
        return (b, z * nx + lax.rem(x + d, nx))

    def z_peer(d):
        return (b, lax.rem(t + nx * d, n_t))

    def plane_peer(d):
        return (lax.rem(b + d // nx, n_b), z * nx + lax.rem(x + lax.rem(d, nx), nx))

    n_plane = n_b * nx - 1
    barrier = pltpu.get_barrier_semaphore()

    def greet(device):
        pl.semaphore_signal(barrier, inc=1, device_id=device, device_id_type=MESH)

    loop(n_plane, lambda d: greet(plane_peer(d + 1)))
    loop(nz - 1, lambda d: greet(z_peer(d + 1)))
    for db_ in (-1, 0, 1):
        for dt_ in (-1, 1):
            greet((band_at(db_), tile_at(dt_)))

    has_n = (b > 0).astype(F32)
    has_s = (b < n_b - 1).astype(F32)
    has_w = (t > 0).astype(F32)
    has_e = (t < n_t - 1).astype(F32)

    def lane_of(rows):
        return lax.broadcasted_iota(jnp.int32, (rows, 128), 1)

    def pack(vO, vH, sbe):
        rows = vO.shape[1]
        lane = lane_of(rows)
        west_half = lane >= 64
        group = lane // 8
        zero = jnp.zeros((rows, 128), F32)

        def half(first_slot, first_row):
            def body(n, carry):
                tw, te = carry
                slot = first_slot + n
                row = first_row + n
                o = vO[row]
                h = vH[row]
                shift = lax.rem(8 * slot + 4, 128)
                here = group == slot
                w = pltpu.roll(jnp.where(west_half, h, o), shift, 1)
                e = pltpu.roll(jnp.where(west_half, o, h), shift, 1)
                return tw + jnp.where(here, w, 0.0), te + jnp.where(here, e, 0.0)

            return loop(ext // 2, body, (zero, zero), unroll=ext // 2)

        tw0, te0 = half(2, 0)
        tw1, te1 = half(0, ext // 2)
        for n in range(6):
            sbe[n] = vO[n]
            sbe[8 + n] = vO[ext - 6 + n]
        sbe[6] = tw0
        sbe[7] = te0
        sbe[14] = tw1
        sbe[15] = te1
        sbe[16] = te0
        sbe[17] = te1
        sbe[18] = tw0
        sbe[19] = tw1

    def send_eight(sbe, rbe, ssem, rsem):
        for first, count, to, db_, dt_ in (
            (16, 1, 22, -1, 1),
            (17, 1, 20, 1, 1),
            (18, 1, 23, -1, -1),
            (19, 1, 21, 1, -1),
            (16, 2, 18, 0, 1),
            (18, 2, 16, 0, -1),
            (0, 8, 8, -1, 0),
            (8, 8, 0, 1, 0),
        ):
            pltpu.make_async_remote_copy(
                src_ref=sbe.at[pl.ds(first, count)],
                dst_ref=rbe.at[pl.ds(to, count)],
                send_sem=ssem,
                recv_sem=rsem,
                device_id=(band_at(db_), tile_at(dt_)),
                device_id_type=MESH,
            ).start()

    def assemble(vO, sbe, rbe, rsem, emit):
        rows = vO.shape[1]
        lane = lane_of(rows)
        pltpu.make_async_copy(rbe, rbe, rsem).wait()
        low = jnp.where(lane < 48, 1.0, 0.0)
        high = jnp.where(lane >= 80, 1.0, 0.0)
        m_w = jnp.where(lane >= 124, has_w, 0.0)
        m_e = jnp.where(lane < 4, has_e, 0.0)

        def turned(slot):
            return pltpu.roll(rbe[slot], 64, 1)

        pw = (
            sbe[18] + has_w * rbe[18] + (has_n * low) * (turned(6) + has_w * turned(20)),
            sbe[19] + has_w * rbe[19] + (has_s * high) * (turned(14) + has_w * turned(22)),
        )
        pe = (
            sbe[16] + has_e * rbe[16] + (has_n * low) * (turned(7) + has_e * turned(21)),
            sbe[17] + has_e * rbe[17] + (has_s * high) * (turned(15) + has_e * turned(23)),
        )

        def finish(o, slot, half, scale, i):
            shift = lax.rem(124 - 8 * slot + 128, 128)
            w = pltpu.roll(pw[half], shift, 1)
            e = pltpu.roll(pe[half], shift, 1)
            o = jnp.where(lane < 4, w, jnp.where(lane >= 124, e, o))
            h = w * m_w + e * m_e
            if scale is not None:
                o = o * scale
                h = h * scale
            emit(i, o, h)

        for i in range(6):
            o = has_n * rbe[i]
            if i >= 2:
                o = o + vO[i - 2]
            finish(o, i, 0, has_n if i < M4 else None, i)
        mid0 = 10
        mid1 = full - 6 - 16

        def body0(n):
            finish(vO[4 + n], 6 + n, 0, None, 6 + n)

        def body1(n):
            finish(vO[14 + n], n, 1, None, 16 + n)

        loop(mid0, body0, unroll=mid0)
        loop(mid1, body1, unroll=mid1)
        for n in range(6):
            i = full - 6 + n
            o = has_s * rbe[8 + n]
            if i < full - 2:
                o = o + vO[i - 2]
            finish(o, i - 16, 1, has_s if i >= full - M4 else None, i)

    def restrict(first, count, acc):
        def body(n, acc):
            row = first + n
            both = halves(FO[row + W])
            part = dot_nt(both, pb[row])
            part = part[0:cols] + part[cols:] + dot_nt(both[0:cols], pb2[row])
            pick = picks[row]
            return tuple(acc[m] + part * (pick == m).astype(F32) for m in range(NCB))

        return loop(count, body, acc, unroll=count)

    def send_x(k):
        for d in far_first(nx):
            pltpu.make_async_remote_copy(
                src_ref=qa.at[k],
                dst_ref=qar.at[k, d - 1],
                send_sem=qasem_s.at[k],
                recv_sem=qasem_r.at[k],
                device_id=x_peer(d),
                device_id_type=MESH,
            ).start()

    def dots_send(k, gamma, delta, eps):
        lane = lane_of(cols)
        g = jnp.sum(gamma, axis=1, keepdims=True)
        d = jnp.sum(delta, axis=1, keepdims=True)
        e = jnp.sum(eps, axis=1, keepdims=True)
        tile = (
            jnp.where(lane == 0, g, 0.0) + jnp.where(lane == 1, d, 0.0) + jnp.where(lane == 2, e, 0.0)
        )
        da[k] = tile[0:8] + pltpu.roll(tile[8:16], 64, 1)

        def send(d):
            pltpu.make_async_remote_copy(
                src_ref=da.at[k],
                dst_ref=dar.at[k, d],
                send_sem=dasem_s.at[k],
                recv_sem=dasem_r.at[k],
                device_id=plane_peer(d + 1),
                device_id_type=MESH,
            ).start()

        def hops(d):
            dy, dx = (d // nx) // 2, d % nx
            return min(dy, n_b // 2 - dy) + min(dx, nx - dx)

        for d in sorted(range(1, n_plane + 1), key=lambda d: -hops(d)):
            send(d - 1)

    def reduce_mid(k):
        pltpu.make_async_copy(qar.at[k], qar.at[k], qasem_r.at[k]).wait()
        for m in range(NCB):
            total = qa[k, m]
            for d in range(nx - 1):
                total = total + qar[k, d, m]
            qb[k, m] = total.astype(BF16)

        def send_q(d):
            pltpu.make_async_remote_copy(
                src_ref=qb.at[k],
                dst_ref=qbr.at[k, d],
                send_sem=qbsem_s.at[k],
                recv_sem=qbsem_r.at[k],
                device_id=z_peer(d + 1),
                device_id_type=MESH,
            ).start()

        for d in far_first(nz):
            send_q(d - 1)

    def dots_mid(k):
        pltpu.make_async_copy(dar.at[k], dar.at[k], dasem_r.at[k]).wait()
        total = da[k]
        for d in range(n_plane):
            total = total + dar[k, d]
        db[k] = total

        def send_d(d):
            pltpu.make_async_remote_copy(
                src_ref=db.at[k],
                dst_ref=dbr.at[k, d],
                send_sem=dbsem_s.at[k],
                recv_sem=dbsem_r.at[k],
                device_id=z_peer(d + 1),
                device_id_type=MESH,
            ).start()

        for d in far_first(nz):
            send_d(d - 1)

    def reduce_end(k):
        pltpu.make_async_copy(qbr.at[k], qbr.at[k], qbsem_r.at[k]).wait()
        for m in range(NCB):
            total = qb[k, m].astype(F32)
            for d in range(nz - 1):
                total = total + qbr[k, d, m].astype(F32)
            yw[m] = total

    def dots_end(k):
        pltpu.make_async_copy(dbr.at[k], dbr.at[k], dbsem_r.at[k]).wait()
        total = db[k]
        for d in range(nz - 1):
            total = total + dbr[k, d]
        tile = jnp.concatenate([total, pltpu.roll(total, 64, 1)], axis=0)
        shape = (cols, 128)
        return tuple(jnp.broadcast_to(tile[:, n : n + 1], shape) for n in range(3))

    def local_solve(between):
        lane = lane_of(cols)
        zero = jnp.zeros((cols, 128), F32)

        def flatten(j, carry):
            s = 4 * j + W
            o = pltpu.roll(FO[j], s, 1)
            h = pltpu.roll(FH[j], s, 1)
            late = lane >= s
            xin[j] = (jnp.where(late, o, h) + carry).astype(BF16)
            return jnp.where(late, h, o)

        tail = loop(ext, flatten, zero, unroll=ext)
        xin[ext] = tail.astype(BF16)

        def inner(n, acc):
            acc = acc * tab[2, n].astype(F32) + dot_nt(xin[tab[1, n]], fac[tab[0, n]])
            run[n] = acc
            return acc

        loop(nb_blocks, inner, zero, unroll=nb_blocks)

        def gather(i):
            gin[i] = run[tab[3, i]].astype(BF16)

        loop(kt, gather, unroll=kt)

        def outer(n, acc):
            acc = acc * tab[6, n].astype(F32) + dot_nn(gin[tab[5, n]], fac[tab[4, n]])
            run[n] = acc
            return acc

        loop(nb_blocks, outer, zero, unroll=nb_blocks)
        between()

        def unflatten(j, carry):
            s = 4 * j + W
            following = run[tab[7, j + 1]]
            here = pltpu.roll(carry, 128 - s, 1)
            there = pltpu.roll(following, 128 - s, 1)
            VO[j] = jnp.where(lane < 128 - s, here, there)
            VH[j] = jnp.where(lane >= 126, here, jnp.where(lane < 2, there, 0.0))
            return following

        loop(ext, unflatten, run[tab[7, 0]], unroll=ext)

    def near(value):
        lane = lane_of(cols)
        return jnp.where((lane < W) | (lane >= 128 - W), value, 0.0)

    def spread_out(row):
        return jnp.broadcast_to(row, (128, 128))

    lane128 = lane_of(128)
    sub128 = lax.broadcasted_iota(jnp.int32, (128, 128), 0)

    def sort_list(first, keys, others):
        keys_sub = jnp.transpose(spread_out(keys))
        others_sub = jnp.transpose(spread_out(others))
        key_lane = spread_out(keys) * 128 + lane128
        key_sub = keys_sub * 128 + sub128
        rank = jnp.sum((key_lane < key_sub).astype(jnp.int32), axis=1, keepdims=True)
        place = rank == lane128

        def put(values):
            return jnp.sum(jnp.where(place, values, 0), axis=0, keepdims=True)

        ordered = put(keys_sub)
        before = pltpu.roll(ordered, 1, 1)
        same = jnp.where((ordered == before) & (lane128[0:1] > 0), 1, 0)
        tabv[first : first + 1, :] = put(sub128)
        tabv[first + 1 : first + 2, :] = put(others_sub)
        tabv[first + 2 : first + 3, :] = same
        tabv[first + 3 : first + 4, :] = (
            jnp.sum((keys_sub <= lane128).astype(jnp.int32), axis=0, keepdims=True) - 1
        )

    lists[...] = jnp.full(lists.shape, 100, jnp.int32)
    loads[0].wait()
    loads[1].wait()
    lists[0:1, 0:nb_blocks] = r["br"][0]
    lists[1:2, 0:nb_blocks] = r["bc"][0]
    sort_list(0, lists[0:1, :], lists[1:2, :])
    sort_list(4, lists[1:2, :], lists[0:1, :])
    to_smem = pltpu.make_async_copy(tabv, tab, insem.at[7])
    to_smem.start()

    rows24 = cols + 8
    zero24 = jnp.zeros((rows24, 128), F32)
    zero = jnp.zeros((cols, 128), F32)
    lane16 = lane_of(cols)
    for row in (0, 1, ext - 2, ext - 1):
        iVO[row] = zero24
    iVH[...] = jnp.zeros(iVH.shape, F32)
    for ref in (UO, UH, MsO, MsH, S, Pp):
        ref[...] = jnp.zeros(ref.shape, F32)
    prev[...] = jnp.ones(prev.shape, F32)
    prev[2] = jnp.full((cols, 128), -1.0, F32)
    prev[3] = zero

    loads[2].wait()
    loads[3].wait()
    for row in range(own):
        value = rs[:, row, :]
        r_out[row] = value
        FO[row + W] = value
        x_out[row] = zero
        iVO[W + row, 0:cols] = value
        iVO[W + row, cols:rows24] = jnp.broadcast_to(co[row : row + 1, :], (8, 128))
    pack(iVO, iVH, isb)

    loads[4].wait()

    def to_bf16(row):
        value = pf[row]
        high = value.astype(BF16)
        pb[row] = high
        pb2[row] = (value - high.astype(F32)).astype(BF16)

    loop(own, to_bf16, unroll=4)
    acc = restrict(0, own, (zero,) * NCB)
    for m in range(NCB):
        qa[0, m] = acc[m]

    group128 = lane128 // 8
    group8 = group128[0:8]
    sub8 = sub128[0:8]
    for half, first_slot, first_row in ((0, M4, 0), (1, 0, 16 - M4)):

        def columns(n, carry):
            slot = first_slot + n
            turned = pltpu.roll(pf[first_row + n], lax.rem(8 * slot + 4, 128), 1)
            chosen = (group8 == slot) & (sub8 == picks[first_row + n])
            return (
                carry[0] + jnp.where(group128 == slot, turned, 0.0),
                carry[1] + jnp.where(chosen, 1.0, 0.0),
            )

        values, masks = loop(
            own // 2, columns, (jnp.zeros((128, 128), F32), jnp.zeros((8, 128), F32)), unroll=4
        )
        pht[half, 0:128] = values
        pht[half, 128:136] = masks

    pl.semaphore_wait(barrier, n_plane + nz - 1 + 6)
    send_eight(isb, irb, exsem_s.at[0], exsem_r.at[0])
    send_x(0)
    loads[5].wait()
    for m in range(NCB):
        value = lax.dot_general(
            cf[:, m * 128 : (m + 1) * 128],
            cf[...],
            (((0,), (0,)), ((), ())),
            precision=lax.Precision.HIGHEST,
            preferred_element_type=F32,
        )
        high = value.astype(BF16)
        bmat[m * 128 : (m + 1) * 128, :] = high
        bmat2[m * 128 : (m + 1) * 128, :] = (value - high.astype(F32)).astype(BF16)

    def take_first(i, o, h):
        if isinstance(i, int):
            keep = W <= i < full - W
        else:
            keep = True
        if keep:
            FO[i - W] = o[0:cols]
            FH[i - W] = near(h[0:cols])
        inside = 0.25
        if isinstance(i, int):
            if i < M4:
                inside = 0.25 * has_n
            elif i >= full - M4:
                inside = 0.25 * has_s
        lane8 = lane16[0:8]
        side = jnp.where(lane8 >= 128 - M4, has_w, 0.0) + jnp.where(lane8 < M4, has_e, 0.0)
        c4O[i] = (o[cols:rows24] + 4.0) * inside
        c4H[i] = (h[cols:rows24] + 4.0) * (side * inside)

    assemble(iVO, isb, irb, exsem_r.at[0], take_first)
    for n, d in enumerate((1, -1)):
        pltpu.make_async_remote_copy(
            src_ref=pht,
            dst_ref=phr.at[n],
            send_sem=phsem_s.at[n],
            recv_sem=phsem_r.at[n],
            device_id=(b, tile_at(d)),
            device_id_type=MESH,
        ).start()

    reduce_mid(0)
    loads[6].wait()
    to_smem.wait()

    side16 = jnp.where(lane16 >= 128 - M4, has_w, 0.0) + jnp.where(lane16 < M4, has_e, 0.0)
    last_lane = lane16 == 127
    first_lane = lane16 == 0

    def row_scale(i):
        north = jnp.where(i < M4, has_n, 1.0)
        south = jnp.where(i >= full - M4, has_s, 1.0)
        return 0.25 * north * south

    def apply_row(srcO, srcH, i):
        o = srcO[i]
        h = srcH[i]
        ol = pltpu.roll(o, 1, 1)
        hl = pltpu.roll(h, 1, 1)
        orr = pltpu.roll(o, 127, 1)
        hr = pltpu.roll(h, 127, 1)
        around_o = (
            srcO[i - 1]
            + srcO[i + 1]
            + jnp.where(first_lane, hl, ol)
            + jnp.where(last_lane, hr, orr)
        )
        around_h = (
            srcH[i - 1]
            + srcH[i + 1]
            + jnp.where(first_lane, ol, hl)
            + jnp.where(last_lane, orr, hr)
        )
        scale = row_scale(i)
        co_ = jnp.concatenate([c4O[i], c4O[i]], axis=0)
        ch_ = jnp.concatenate([c4H[i], c4H[i]], axis=0)
        return co_ * o - scale * around_o, ch_ * h - (scale * side16) * around_h

    def once(i):
        o, h = apply_row(UO, UH, i)
        AO[i] = o
        AH[i] = h

    def twice(i):
        o, h = apply_row(AO, AH, i)
        FO[i - W] = o
        FH[i - W] = near(h)

    def lift(first, count):
        def body(n):
            row = first + n
            both = zcat[picks[row]]
            part = dot_nn(both, pb[row])
            LV[row] = part[0:cols] + part[cols:] + dot_nn(both[0:cols], pb2[row])

        loop(count, body, unroll=count)

    def leave(n):
        return pltpu.make_async_copy(
            r[("xst2", "rst2", "ust")[n]], r[("x_out", "r_out", "u_out")[n]], r["outsem"].at[n]
        )

    def stage(k, carry):
        def between():
            @pl.when(k > 0)
            def _():
                reduce_mid(k)

        local_solve(between)
        pack(VO, VH, sb.at[k])
        send_eight(sb.at[k], rb.at[k], exsem_s.at[1 + k], exsem_r.at[1 + k])

        @pl.when(k > 0)
        def _():
            dots_mid(k)

        @pl.when(k == 0)
        def _():
            for n in range(2):
                pltpu.make_async_copy(phr.at[n], phr.at[n], phsem_r.at[n]).wait()
            from_west = lax.rem(lane128, 8) < M4
            for half in range(2):
                value = jnp.where(from_west, has_w * phr[0, half, 0:128], has_e * phr[1, half, 0:128])
                high = value.astype(BF16)
                ph[half] = high
                ph2[half] = (value - high.astype(F32)).astype(BF16)
                pm[half] = jnp.where(from_west[0:8], phr[0, half, 128:136], phr[1, half, 128:136])

        reduce_end(k)

        solved = jnp.zeros((cols, NCB * 128), F32)
        for m in range(NCB):
            both = halves(yw[m])
            part = dot_nn(both, bmat[m * 128 : (m + 1) * 128, :])
            solved = solved + part[0:cols] + part[cols:]
            solved = solved + dot_nn(both[0:cols], bmat2[m * 128 : (m + 1) * 128, :])
        for m in range(NCB):
            zcat[m] = halves(solved[:, m * 128 : (m + 1) * 128])
        lift(0, M4)
        lift(own - M4, M4)
        for half in range(2):
            total = zero
            for m in range(NCB):
                both = zcat[m]
                part = dot_nn(both, ph[half])
                part = part[0:cols] + part[cols:] + dot_nn(both[0:cols], ph2[half])
                total = total + part * jnp.broadcast_to(pm[half, m : m + 1, :], (cols, 128))
            pk[half] = total

        @pl.when(k < STAGES - 1)
        def _():
            for n in range(M4):
                nsb[k, n] = LV[n]
                nsb[k, M4 + 1 + n] = LV[own - M4 + n]
            nsb[k, M4] = pk[0]
            nsb[k, 2 * M4 + 1] = pk[1]
            for first, to, d in ((0, M4 + 1, -1), (M4 + 1, 0, 1)):
                pltpu.make_async_remote_copy(
                    src_ref=nsb.at[k, pl.ds(first, M4 + 1)],
                    dst_ref=nrb.at[k, pl.ds(to, M4 + 1)],
                    send_sem=nssem_s.at[k],
                    recv_sem=nssem_r.at[k],
                    device_id=(band_at(d), t),
                    device_id_type=MESH,
                ).start()

        lift(M4, own - 2 * M4)

        def keep(i, o, h):
            TO[i] = o
            TH[i] = h

        assemble(VO, sb.at[k], rb.at[k], exsem_r.at[1 + k], keep)

        @pl.when(k > 0)
        def _():
            g, d, e = dots_end(k)
            beta = jnp.where(k > 1, g / prev[0], 0.0)
            curv = jnp.where(k > 1, d + 2.0 * beta * e + beta * beta * prev[1], d)
            alpha = g / curv
            prev[0] = g
            prev[1] = curv
            prev[2] = alpha
            prev[3] = beta

            def body(row):
                p = UO[row + M4] + beta * Pp[row]
                s = FO[row + W] + beta * S[row]
                Pp[row] = p
                S[row] = s
                x_out[row] = x_out[row] + alpha * p
                r_out[row] = r_out[row] - alpha * s

            loop(own, body, unroll=own)

        @pl.when(k == STAGES - 1)
        def _():
            def body(row):
                r["xst2"][:, row, :] = x_out[row]
                r["rst2"][:, row, :] = r_out[row]

            loop(own, body, unroll=own)
            leave(0).start()
            leave(1).start()

        alpha = prev[2]
        beta = prev[3]

        def combine(i, o, h):
            ms = TO[i] + o + beta * MsO[i]
            MsO[i] = ms
            UO[i] = UO[i] - alpha * ms
            ms = TH[i] + h + beta * MsH[i]
            MsH[i] = ms
            UH[i] = UH[i] - alpha * ms

        for half, first_slot, first_row in ((0, M4, 0), (1, 0, 16 - M4)):
            strip = pk[half]

            def inner_rows(n):
                slot = first_slot + n
                h = pltpu.roll(strip, lax.rem(252 - 8 * slot, 128), 1) * side16
                combine(16 * half + slot, LV[first_row + n], h)

            loop(own // 2, inner_rows, unroll=own // 2)

        @pl.when(k < STAGES - 1)
        def _():
            loop(full - 10, lambda n: once(5 + n), unroll=full - 10)
            loop(full - 12, lambda n: twice(6 + n), unroll=full - 12)
            acc = restrict(2, own - 4, (zero,) * NCB)

            pltpu.make_async_copy(nrb.at[k], nrb.at[k], nssem_r.at[k]).wait()
            for n in range(M4):
                combine(n, nrb[k, n] * has_n, pltpu.roll(nrb[k, M4], 60 - 8 * n, 1) * (has_n * side16))
                combine(
                    full - M4 + n,
                    nrb[k, M4 + 1 + n] * has_s,
                    pltpu.roll(nrb[k, 2 * M4 + 1], 92 - 8 * n, 1) * (has_s * side16),
                )
            for n in range(4):
                once(1 + n)
                once(full - 5 + n)
            for n in range(4):
                twice(2 + n)
                twice(full - 6 + n)
            acc = restrict(0, 2, acc)
            acc = restrict(own - 2, 2, acc)
            for m in range(NCB):
                qa[k + 1, m] = acc[m]
            send_x(k + 1)

            def dots(row, acc):
                u = UO[row + M4]
                return (
                    acc[0] + u * r_out[row],
                    acc[1] + u * FO[row + W],
                    acc[2] + u * S[row],
                )

            dots_send(k + 1, *loop(own, dots, (zero, zero, zero), unroll=own))

        @pl.when(k == STAGES - 1)
        def _():
            def body(row):
                r["ust"][:, row, :] = UO[row + M4]

            loop(own, body, unroll=own)
            leave(2).start()

        return carry

    lax.fori_loop(0, STAGES, stage, 0)

    pltpu.make_async_copy(irb, irb, exsem_s.at[0]).wait()

    def sent(e):
        pltpu.make_async_copy(rb.at[e], rb.at[e], exsem_s.at[1 + e]).wait()

    loop(STAGES, sent)
    for n in range(2):
        pltpu.make_async_copy(phr.at[n], phr.at[n], phsem_s.at[n]).wait()

    def sent_ns(k):
        pltpu.make_async_copy(nrb.at[k], nrb.at[k], nssem_s.at[k]).wait()

    loop(STAGES - 1, sent_ns)

    def sent_q(k):
        pltpu.make_async_copy(qar.at[k], qar.at[k], qasem_s.at[k]).wait()
        pltpu.make_async_copy(qbr.at[k], qbr.at[k], qbsem_s.at[k]).wait()

    loop(STAGES, sent_q)

    def sent_d(k):
        pltpu.make_async_copy(dar.at[k + 1], dar.at[k + 1], dasem_s.at[k + 1]).wait()
        pltpu.make_async_copy(dbr.at[k + 1], dbr.at[k + 1], dbsem_s.at[k + 1]).wait()

    loop(STAGES - 1, sent_d)
    for n in range(3):
        leave(n).wait()


def local(n_b, n_t, right_side, coeff_field, factor_blocks, block_rows, block_cols, prolong, coarse_picks, coarse_factor):
    cols, lat, lon = right_side.shape
    count = factor_blocks.shape[2]
    ext = lat + 2 * W
    full = lat + 2 * M4
    kt = (ext * (lon + 2 * W) + 127) // 128
    nx = 4 if n_t % 4 == 0 and n_t > 4 else 2
    nz = n_t // nx
    cfg = (n_b, n_t, nx, nz, lat, count, kt, cols)
    n_plane = n_b * nx - 1
    rows24 = cols + 8
    vm = pltpu.VMEM
    ext_f = vm((ext, cols, 128), F32)
    full_f = vm((full, cols, 128), F32)
    own_f = vm((lat, cols, 128), F32)
    cn = coarse_factor.shape[1:]
    four = vm((NCB, cols, 128), F32)
    dma = pltpu.SemaphoreType.DMA
    scratch = dict(
        tab=pltpu.SMEM((8, 128), jnp.int32),
        tabv=vm((8, 128), jnp.int32),
        lists=vm((8, 128), jnp.int32),
        br=vm((1, 1, count), jnp.int32),
        bc=vm((1, 1, count), jnp.int32),
        rs=vm((cols, lat, lon), F32),
        co=vm((lat, lon), F32),
        fac=vm((count, 128, 128), BF16),
        pf=vm((lat, 128, 128), F32),
        cf=vm(cn, F32),
        pb=vm((lat, 128, 128), BF16),
        pb2=vm((lat, 128, 128), BF16),
        bmat=vm(cn, BF16),
        bmat2=vm(cn, BF16),
        zcat=vm((NCB, 2 * cols, 128), BF16),
        iVO=vm((ext, rows24, 128), F32),
        iVH=vm((ext, rows24, 128), F32),
        isb=vm((24, rows24, 128), F32),
        irb=vm((24, rows24, 128), F32),
        VO=ext_f,
        VH=ext_f,
        sb=vm((STAGES, 24, cols, 128), F32),
        rb=vm((STAGES, 24, cols, 128), F32),
        LV=own_f,
        pk=vm((2, cols, 128), F32),
        nsb=vm((ITERS, 2 * M4 + 2, cols, 128), F32),
        nrb=vm((ITERS, 2 * M4 + 2, cols, 128), F32),
        pht=vm((2, 136, 128), F32),
        phr=vm((2, 2, 136, 128), F32),
        ph=vm((2, 128, 128), BF16),
        ph2=vm((2, 128, 128), BF16),
        pm=vm((2, 8, 128), F32),
        UO=full_f,
        UH=full_f,
        AO=full_f,
        AH=full_f,
        FO=ext_f,
        FH=ext_f,
        c4O=vm((full, 8, 128), F32),
        c4H=vm((full, 8, 128), F32),
        MsO=full_f,
        MsH=full_f,
        TO=full_f,
        TH=full_f,
        xst2=vm((cols, lat, 128), F32),
        rst2=vm((cols, lat, 128), F32),
        ust=vm((cols, lat, 128), F32),
        outsem=dma((3,)),
        xst=own_f,
        rst=own_f,
        S=own_f,
        Pp=own_f,
        yw=four,
        xin=vm((kt, cols, 128), BF16),
        gin=vm((kt, cols, 128), BF16),
        run=vm((count, cols, 128), F32),
        prev=vm((4, cols, 128), F32),
        qa=vm((STAGES, NCB, cols, 128), F32),
        qar=vm((STAGES, nx - 1, NCB, cols, 128), F32),
        qb=vm((STAGES, NCB, cols, 128), BF16),
        qbr=vm((STAGES, nz - 1, NCB, cols, 128), BF16),
        da=vm((STAGES, 8, 128), F32),
        dar=vm((STAGES, n_plane, 8, 128), F32),
        db=vm((STAGES, 8, 128), F32),
        dbr=vm((STAGES, nz - 1, 8, 128), F32),
        insem=dma((8,)),
        exsem_s=dma((1 + STAGES,)),
        exsem_r=dma((1 + STAGES,)),
        nssem_s=dma((ITERS,)),
        nssem_r=dma((ITERS,)),
        phsem_s=dma((2,)),
        phsem_r=dma((2,)),
    )
    for name in ("qasem_s", "qasem_r", "qbsem_s", "qbsem_r", "dasem_s", "dasem_r", "dbsem_s", "dbsem_r"):
        scratch[name] = dma((STAGES,))
    inputs = dict(
        picks=coarse_picks.reshape(lat),
        br_hbm=block_rows.reshape(1, 1, count),
        bc_hbm=block_cols.reshape(1, 1, count),
        rs_hbm=right_side,
        co_hbm=coeff_field,
        f_hbm=factor_blocks.reshape(factor_blocks.shape[2:]),
        p_hbm=prolong.reshape(lat, 128, lon),
        c_hbm=coarse_factor.reshape(cn),
    )
    results = ("x_out", "r_out", "u_out")
    out = jax.ShapeDtypeStruct((cols, lat, 128), F32)
    outs = pl.pallas_call(
        functools.partial(kernel, cfg, tuple(inputs) + results + tuple(scratch)),
        out_shape=(out, out, out),
        in_specs=[pl.BlockSpec(memory_space=pltpu.SMEM)]
        + [pl.BlockSpec(memory_space=pltpu.HBM)] * (len(inputs) - 1),
        out_specs=(pl.BlockSpec(memory_space=pltpu.HBM),) * 3,
        scratch_shapes=list(scratch.values()),
        compiler_params=pltpu.CompilerParams(
            collective_id=3, has_side_effects=True, vmem_limit_bytes=63 << 20
        ),
    )(*inputs.values())

    def hand_on(*refs):
        for n in range(3):
            refs[3 + n][...] = refs[n][...]

    return pl.pallas_call(
        hand_on,
        out_shape=(out, out, out),
    )(*outs)


def solution(mesh):
    in_specs = (
        P(None, "band", "tile"),
        P("band", "tile"),
        P("band", "tile", None, None, None),
        P("band", "tile", None),
        P("band", "tile", None),
        P("band", None, None, "tile"),
        P("band", "tile", None),
        P("band", None, None),
    )
    out_specs = (P(None, "band", "tile"),) * 3
    return jax.shard_map(
        functools.partial(local, mesh.shape["band"], mesh.shape["tile"]),
        mesh=mesh,
        in_specs=in_specs,
        out_specs=out_specs,
        check_vma=False,
    )
```

```python
import functools

import jax
import jax.numpy as jnp
from jax import lax
from jax.experimental import pallas as pl
from jax.experimental.pallas import tpu as pltpu
from jax.sharding import PartitionSpec as P

MESH = pl.DeviceIdType.MESH
W = 2
NCB = 4
ITERS = 3
STAGES = ITERS + 1
M4 = 4
F32 = jnp.float32
BF16 = jnp.bfloat16


def loop(count, body, init=None, unroll=1):
    if init is None:

        def step(i, carry):
            body(i)
            return carry

        return lax.fori_loop(0, count, step, 0, unroll=unroll)
    return lax.fori_loop(0, count, body, init, unroll=unroll)


def dot_nn(a, b):
    return lax.dot_general(a, b, (((1,), (0,)), ((), ())), preferred_element_type=F32)


def dot_nt(a, b):
    return lax.dot_general(a, b, (((1,), (1,)), ((), ())), preferred_element_type=F32)


def far_first(count):
    return sorted(range(1, count), key=lambda d: -min(d, count - d))


def halves(value):
    high = value.astype(BF16)
    low = (value - high.astype(F32)).astype(BF16)
    return jnp.concatenate([high, low], axis=0)


def kernel(cfg, names, *refs):
    r = dict(zip(names, refs))
    rs_hbm, co_hbm, f_hbm, p_hbm, c_hbm = (r[n] for n in ("rs_hbm", "co_hbm", "f_hbm", "p_hbm", "c_hbm"))
    x_out, r_out = r["xst"], r["rst"]
    picks, tab, tabv, lists = r["picks"], r["tab"], r["tabv"], r["lists"]
    rs, co, fac, pf, cf = r["rs"], r["co"], r["fac"], r["pf"], r["cf"]
    facT = r["facT"]
    pb, pb2, bmat, bmat2, zcat = r["pb"], r["pb2"], r["bmat"], r["bmat2"], r["zcat"]
    iVO, iVH, isb, irb = r["iVO"], r["iVH"], r["isb"], r["irb"]
    cVO, cVH, csb, crb = r["cVO"], r["cVH"], r["csb"], r["crb"]
    VO, VH, sb, rb = r["VO"], r["VH"], r["sb"], r["rb"]
    LV, pk, nsb, nrb = r["LV"], r["pk"], r["nsb"], r["nrb"]
    pht, phr, ph, ph2, pm = r["pht"], r["phr"], r["ph"], r["ph2"], r["pm"]
    UO, UH, AO, AH, FO, FH = r["UO"], r["UH"], r["AO"], r["AH"], r["FO"], r["FH"]
    c4O, c4H, MsO, MsH, TO, TH = r["c4O"], r["c4H"], r["MsO"], r["MsH"], r["TO"], r["TH"]
    S, Pp, yw, xin, gin, run, prev = r["S"], r["Pp"], r["yw"], r["xin"], r["gin"], r["run"], r["prev"]
    qa, qar, qb, qbr = r["qa"], r["qar"], r["qb"], r["qbr"]
    da, dar, db, dbr = r["da"], r["dar"], r["db"], r["dbr"]
    insem, exsem_s, exsem_r = r["insem"], r["exsem_s"], r["exsem_r"]
    nssem_s, nssem_r, phsem_s, phsem_r = r["nssem_s"], r["nssem_r"], r["phsem_s"], r["phsem_r"]
    qasem_s, qasem_r, qbsem_s, qbsem_r = r["qasem_s"], r["qasem_r"], r["qbsem_s"], r["qbsem_r"]
    dasem_s, dasem_r, dbsem_s, dbsem_r = r["dasem_s"], r["dasem_r"], r["dbsem_s"], r["dbsem_r"]
    n_b, n_t, nx, nz, lat, nb_blocks, kt, cols = cfg
    b = lax.axis_index("band")
    t = lax.axis_index("tile")
    z = t // nx
    x = t % nx
    own = lat
    ext = lat + 2 * W
    full = lat + 2 * M4

    sources = (r["br_hbm"], r["bc_hbm"], rs_hbm, co_hbm, p_hbm, c_hbm, f_hbm)
    targets = (r["br"], r["bc"], rs, co, pf, cf, fac)
    loads = [pltpu.make_async_copy(a, c, insem.at[n]) for n, (a, c) in enumerate(zip(sources, targets))]
    bands = [lax.rem(b + d, n_b) for d in range(n_b)]
    tiles_x = [z * nx + lax.rem(x + d, nx) for d in range(nx)]
    tiles_z = [lax.rem(t + nx * d, n_t) for d in range(nz)]
    tiles_next = {1: lax.rem(t + 1, n_t), -1: lax.rem(t + n_t - 1, n_t), 0: t}

    def band_at(d):
        return bands[d % n_b]

    def tile_at(d):
        return tiles_next[d]

    def x_peer(d):
        return (b, tiles_x[d])

    def z_peer(d):
        return (b, tiles_z[d])

    def plane_peer(d):
        return (bands[d // nx], tiles_x[d % nx])

    n_plane = n_b * nx - 1
    barrier = pltpu.get_barrier_semaphore()

    def greet(device):
        pl.semaphore_signal(barrier, inc=1, device_id=device, device_id_type=MESH)

    for copy in loads:
        copy.start()
    for d in range(1, n_plane + 1):
        greet(plane_peer(d))
    for d in far_first(nz):
        greet(z_peer(d))
    for db_ in (-1, 0, 1):
        for dt_ in (-1, 1):
            greet((band_at(db_), tile_at(dt_)))


    has_n = (b > 0).astype(F32)
    has_s = (b < n_b - 1).astype(F32)
    has_w = (t > 0).astype(F32)
    has_e = (t < n_t - 1).astype(F32)

    def lane_of(rows):
        return lax.broadcasted_iota(jnp.int32, (rows, 128), 1)

    def pack(vO, vH, sbe):
        rows = vO.shape[1]
        lane = lane_of(rows)
        west_half = lane >= 64
        group = lane // 8
        zero = jnp.zeros((rows, 128), F32)

        def half(first_slot, first_row):
            def body(n, carry):
                tw, te = carry
                slot = first_slot + n
                row = first_row + n
                o = vO[row]
                h = vH[row]
                shift = lax.rem(8 * slot + 4, 128)
                here = group == slot
                w = pltpu.roll(jnp.where(west_half, h, o), shift, 1)
                e = pltpu.roll(jnp.where(west_half, o, h), shift, 1)
                return tw + jnp.where(here, w, 0.0), te + jnp.where(here, e, 0.0)

            return loop(ext // 2, body, (zero, zero), unroll=ext // 2)

        tw0, te0 = half(2, 0)
        tw1, te1 = half(0, ext // 2)
        for n in range(6):
            sbe[n] = vO[n]
            sbe[8 + n] = vO[ext - 6 + n]
        sbe[6] = tw0
        sbe[7] = te0
        sbe[14] = tw1
        sbe[15] = te1
        sbe[16] = te0
        sbe[17] = te1
        sbe[18] = tw0
        sbe[19] = tw1

    def send_eight(sbe, rbe, ssem, rsem):
        for first, count, to, db_, dt_ in (
            (16, 1, 22, -1, 1),
            (17, 1, 20, 1, 1),
            (18, 1, 23, -1, -1),
            (19, 1, 21, 1, -1),
            (16, 2, 18, 0, 1),
            (18, 2, 16, 0, -1),
            (0, 8, 8, -1, 0),
            (8, 8, 0, 1, 0),
        ):
            pltpu.make_async_remote_copy(
                src_ref=sbe.at[pl.ds(first, count)],
                dst_ref=rbe.at[pl.ds(to, count)],
                send_sem=ssem,
                recv_sem=rsem,
                device_id=(band_at(db_), tile_at(dt_)),
                device_id_type=MESH,
            ).start()

    def assemble(vO, sbe, rbe, rsem, emit):
        rows = vO.shape[1]
        lane = lane_of(rows)
        pltpu.make_async_copy(rbe, rbe, rsem).wait()
        low = jnp.where(lane < 48, 1.0, 0.0)
        high = jnp.where(lane >= 80, 1.0, 0.0)
        m_w = jnp.where(lane >= 124, has_w, 0.0)
        m_e = jnp.where(lane < 4, has_e, 0.0)

        def turned(slot):
            return pltpu.roll(rbe[slot], 64, 1)

        pw = (
            sbe[18] + has_w * rbe[18] + (has_n * low) * (turned(6) + has_w * turned(20)),
            sbe[19] + has_w * rbe[19] + (has_s * high) * (turned(14) + has_w * turned(22)),
        )
        pe = (
            sbe[16] + has_e * rbe[16] + (has_n * low) * (turned(7) + has_e * turned(21)),
            sbe[17] + has_e * rbe[17] + (has_s * high) * (turned(15) + has_e * turned(23)),
        )

        def finish(o, slot, half, scale, i):
            shift = lax.rem(124 - 8 * slot + 128, 128)
            w = pltpu.roll(pw[half], shift, 1)
            e = pltpu.roll(pe[half], shift, 1)
            o = jnp.where(lane < 4, w, jnp.where(lane >= 124, e, o))
            h = w * m_w + e * m_e
            if scale is not None:
                o = o * scale
                h = h * scale
            emit(i, o, h)

        for i in range(6):
            o = has_n * rbe[i]
            if i >= 2:
                o = o + vO[i - 2]
            finish(o, i, 0, has_n if i < M4 else None, i)
        mid0 = 10
        mid1 = full - 6 - 16

        def body0(n):
            finish(vO[4 + n], 6 + n, 0, None, 6 + n)

        def body1(n):
            finish(vO[14 + n], n, 1, None, 16 + n)

        loop(mid0, body0, unroll=mid0)
        loop(mid1, body1, unroll=mid1)
        for n in range(6):
            i = full - 6 + n
            o = has_s * rbe[8 + n]
            if i < full - 2:
                o = o + vO[i - 2]
            finish(o, i - 16, 1, has_s if i >= full - M4 else None, i)

    def restrict(first, count, acc):
        def body(n, acc):
            row = first + n
            both = halves(FO[row + W])
            part = dot_nt(both, pb[row])
            part = part[0:cols] + part[cols:] + dot_nt(both[0:cols], pb2[row])
            pick = picks[row]
            return tuple(acc[m] + part * (pick == m).astype(F32) for m in range(NCB))

        return loop(count, body, acc, unroll=count)

    def send_x(k):
        for d in far_first(nx):
            pltpu.make_async_remote_copy(
                src_ref=qa.at[k],
                dst_ref=qar.at[k, d - 1],
                send_sem=qasem_s.at[k],
                recv_sem=qasem_r.at[k],
                device_id=x_peer(d),
                device_id_type=MESH,
            ).start()

    def dots_send(k, gamma, delta, eps):
        lane = lane_of(cols)
        g = jnp.sum(gamma, axis=1, keepdims=True)
        d = jnp.sum(delta, axis=1, keepdims=True)
        e = jnp.sum(eps, axis=1, keepdims=True)
        tile = (
            jnp.where(lane == 0, g, 0.0) + jnp.where(lane == 1, d, 0.0) + jnp.where(lane == 2, e, 0.0)
        )
        da[k] = tile[0:8] + pltpu.roll(tile[8:16], 64, 1)

        def send(d):
            pltpu.make_async_remote_copy(
                src_ref=da.at[k],
                dst_ref=dar.at[k, d],
                send_sem=dasem_s.at[k],
                recv_sem=dasem_r.at[k],
                device_id=plane_peer(d + 1),
                device_id_type=MESH,
            ).start()

        def hops(d):
            dy, dx = (d // nx) // 2, d % nx
            return min(dy, n_b // 2 - dy) + min(dx, nx - dx)

        for d in sorted(range(1, n_plane + 1), key=lambda d: -hops(d)):
            send(d - 1)

    def reduce_mid(k):
        pltpu.make_async_copy(qar.at[k], qar.at[k], qasem_r.at[k]).wait()
        for m in range(NCB):
            total = qa[k, m].astype(F32)
            for d in range(nx - 1):
                total = total + qar[k, d, m].astype(F32)
            qb[k, m] = total.astype(BF16)

        def send_q(d):
            pltpu.make_async_remote_copy(
                src_ref=qb.at[k],
                dst_ref=qbr.at[k, d],
                send_sem=qbsem_s.at[k],
                recv_sem=qbsem_r.at[k],
                device_id=z_peer(d + 1),
                device_id_type=MESH,
            ).start()

        for d in far_first(nz):
            send_q(d - 1)

    def dots_mid(k):
        pltpu.make_async_copy(dar.at[k], dar.at[k], dasem_r.at[k]).wait()
        total = da[k]
        for d in range(n_plane):
            total = total + dar[k, d]
        db[k] = total

        def send_d(d):
            pltpu.make_async_remote_copy(
                src_ref=db.at[k],
                dst_ref=dbr.at[k, d],
                send_sem=dbsem_s.at[k],
                recv_sem=dbsem_r.at[k],
                device_id=z_peer(d + 1),
                device_id_type=MESH,
            ).start()

        for d in far_first(nz):
            send_d(d - 1)

    def reduce_end(k):
        pltpu.make_async_copy(qbr.at[k], qbr.at[k], qbsem_r.at[k]).wait()
        for m in range(NCB):
            total = qb[k, m].astype(F32)
            for d in range(nz - 1):
                total = total + qbr[k, d, m].astype(F32)
            yw[m] = total

    def dots_end(k):
        pltpu.make_async_copy(dbr.at[k], dbr.at[k], dbsem_r.at[k]).wait()
        total = db[k]
        for d in range(nz - 1):
            total = total + dbr[k, d]
        tile = jnp.concatenate([total, pltpu.roll(total, 64, 1)], axis=0)
        shape = (cols, 128)
        return tuple(jnp.broadcast_to(tile[:, n : n + 1], shape) for n in range(3))

    def local_solve(between):
        lane = lane_of(cols)
        zero = jnp.zeros((cols, 128), F32)

        def flatten(j, carry):
            s = 4 * j + W
            o = pltpu.roll(FO[j], s, 1)
            h = pltpu.roll(FH[j], s, 1)
            late = lane >= s
            xin[j] = (jnp.where(late, o, h) + carry).astype(BF16)
            return jnp.where(late, h, o)

        tail = loop(ext, flatten, zero, unroll=ext)
        xin[ext] = tail.astype(BF16)

        def inner(n, acc):
            acc = acc * tab[2, n].astype(F32) + dot_nn(xin[tab[1, n]], facT[tab[0, n]])
            run[n] = acc
            return acc

        loop(nb_blocks, inner, zero, unroll=nb_blocks)

        def gather(i):
            gin[i] = run[tab[3, i]].astype(BF16)

        loop(kt, gather, unroll=kt)

        def outer(n, acc):
            acc = acc * tab[6, n].astype(F32) + dot_nn(gin[tab[5, n]], fac[tab[4, n]])
            run[n] = acc
            return acc

        early = nb_blocks * 5 // 8
        acc = loop(early, outer, zero, unroll=early)
        between()
        loop(nb_blocks - early, lambda n, a: outer(early + n, a), acc, unroll=nb_blocks - early)

        def unflatten(j, carry):
            s = 4 * j + W
            following = run[tab[7, j + 1]]
            here = pltpu.roll(carry, 128 - s, 1)
            there = pltpu.roll(following, 128 - s, 1)
            VO[j] = jnp.where(lane < 128 - s, here, there)
            VH[j] = jnp.where(lane >= 126, here, jnp.where(lane < 2, there, 0.0))
            return following

        loop(ext, unflatten, run[tab[7, 0]], unroll=ext)

    def near(value):
        lane = lane_of(cols)
        return jnp.where((lane < W) | (lane >= 128 - W), value, 0.0)

    def spread_out(row):
        return jnp.broadcast_to(row, (128, 128))

    lane128 = lane_of(128)
    sub128 = lax.broadcasted_iota(jnp.int32, (128, 128), 0)

    def sort_list(first, keys, others):
        keys_sub = jnp.transpose(spread_out(keys))
        others_sub = jnp.transpose(spread_out(others))
        key_lane = spread_out(keys) * 128 + lane128
        key_sub = keys_sub * 128 + sub128
        rank = jnp.sum((key_lane < key_sub).astype(jnp.int32), axis=1, keepdims=True)
        place = rank == lane128

        def put(values):
            return jnp.sum(jnp.where(place, values, 0), axis=0, keepdims=True)

        ordered = put(keys_sub)
        before = pltpu.roll(ordered, 1, 1)
        same = jnp.where((ordered == before) & (lane128[0:1] > 0), 1, 0)
        tabv[first : first + 1, :] = put(sub128)
        tabv[first + 1 : first + 2, :] = put(others_sub)
        tabv[first + 2 : first + 3, :] = same
        tabv[first + 3 : first + 4, :] = (
            jnp.sum((keys_sub <= lane128).astype(jnp.int32), axis=0, keepdims=True) - 1
        )

    lists[...] = jnp.full(lists.shape, 100, jnp.int32)
    loads[0].wait()
    loads[1].wait()
    lists[0:1, 0:nb_blocks] = r["br"][0]
    lists[1:2, 0:nb_blocks] = r["bc"][0]
    sort_list(0, lists[0:1, :], lists[1:2, :])
    sort_list(4, lists[1:2, :], lists[0:1, :])
    to_smem = pltpu.make_async_copy(tabv, tab, insem.at[7])
    to_smem.start()

    zero = jnp.zeros((cols, 128), F32)
    lane16 = lane_of(cols)
    for row in (0, 1, ext - 2, ext - 1):
        iVO[row] = zero
        cVO[row] = zero[0:8]
    for ref in (iVH, cVH, UO, UH, MsO, MsH, S, Pp):
        ref[...] = jnp.zeros(ref.shape, F32)
    prev[...] = jnp.ones(prev.shape, F32)
    prev[2] = jnp.full((cols, 128), -1.0, F32)
    prev[3] = zero

    loads[2].wait()
    loads[3].wait()
    for row in range(own):
        value = rs[:, row, :]
        r_out[row] = value
        FO[row + W] = value
        x_out[row] = zero
        iVO[W + row] = value
        cVO[W + row] = jnp.broadcast_to(co[row : row + 1, :], (8, 128))
    pack(iVO, iVH, isb)
    pack(cVO, cVH, csb)

    loads[4].wait()

    def to_bf16(row):
        value = pf[row]
        high = value.astype(BF16)
        pb[row] = high
        pb2[row] = (value - high.astype(F32)).astype(BF16)

    loop(own, to_bf16, unroll=4)
    acc = restrict(0, own, (zero,) * NCB)
    for m in range(NCB):
        qa[0, m] = acc[m].astype(BF16)

    group128 = lane128 // 8
    group8 = group128[0:8]
    sub8 = sub128[0:8]
    for half, first_slot, first_row in ((0, M4, 0), (1, 0, 16 - M4)):

        def columns(n, carry):
            slot = first_slot + n
            turned = pltpu.roll(pf[first_row + n], lax.rem(8 * slot + 4, 128), 1)
            chosen = (group8 == slot) & (sub8 == picks[first_row + n])
            return (
                carry[0] + jnp.where(group128 == slot, turned, 0.0),
                carry[1] + jnp.where(chosen, 1.0, 0.0),
            )

        values, masks = loop(
            own // 2, columns, (jnp.zeros((128, 128), F32), jnp.zeros((8, 128), F32)), unroll=4
        )
        pht[half, 0:128] = values
        pht[half, 128:136] = masks

    pl.semaphore_wait(barrier, n_plane + nz - 1 + 6)
    send_eight(isb, irb, exsem_s.at[0], exsem_r.at[0])
    send_x(0)
    send_eight(csb, crb, exsem_s.at[1 + STAGES], exsem_r.at[1 + STAGES])
    loads[6].wait()

    def turned(n):
        facT[n] = jnp.transpose(fac[n])

    loop(nb_blocks, turned, unroll=4)
    loads[5].wait()
    for m in range(NCB):
        value = lax.dot_general(
            cf[:, m * 128 : (m + 1) * 128],
            cf[...],
            (((0,), (0,)), ((), ())),
            precision=lax.Precision.HIGHEST,
            preferred_element_type=F32,
        )
        high = value.astype(BF16)
        bmat[m * 128 : (m + 1) * 128, :] = high
        bmat2[m * 128 : (m + 1) * 128, :] = (value - high.astype(F32)).astype(BF16)

    def take_first(i, o, h):
        if isinstance(i, int):
            keep = W <= i < full - W
        else:
            keep = True
        if keep:
            FO[i - W] = o
            FH[i - W] = near(h)

    def take_coefficients(i, o, h):
        inside = 0.25
        if isinstance(i, int):
            if i < M4:
                inside = 0.25 * has_n
            elif i >= full - M4:
                inside = 0.25 * has_s
        lane8 = lane16[0:8]
        side = jnp.where(lane8 >= 128 - M4, has_w, 0.0) + jnp.where(lane8 < M4, has_e, 0.0)
        c4O[i] = (o + 4.0) * inside
        c4H[i] = (h + 4.0) * (side * inside)

    assemble(iVO, isb, irb, exsem_r.at[0], take_first)
    for n, d in enumerate((1, -1)):
        pltpu.make_async_remote_copy(
            src_ref=pht,
            dst_ref=phr.at[n],
            send_sem=phsem_s.at[n],
            recv_sem=phsem_r.at[n],
            device_id=(b, tile_at(d)),
            device_id_type=MESH,
        ).start()

    reduce_mid(0)
    to_smem.wait()

    side16 = jnp.where(lane16 >= 128 - M4, has_w, 0.0) + jnp.where(lane16 < M4, has_e, 0.0)
    last_lane = lane16 == 127
    first_lane = lane16 == 0

    def row_scale(i):
        north = jnp.where(i < M4, has_n, 1.0)
        south = jnp.where(i >= full - M4, has_s, 1.0)
        return 0.25 * north * south

    def apply_row(srcO, srcH, i):
        o = srcO[i]
        h = srcH[i]
        ol = pltpu.roll(o, 1, 1)
        hl = pltpu.roll(h, 1, 1)
        orr = pltpu.roll(o, 127, 1)
        hr = pltpu.roll(h, 127, 1)
        around_o = (
            srcO[i - 1]
            + srcO[i + 1]
            + jnp.where(first_lane, hl, ol)
            + jnp.where(last_lane, hr, orr)
        )
        around_h = (
            srcH[i - 1]
            + srcH[i + 1]
            + jnp.where(first_lane, ol, hl)
            + jnp.where(last_lane, orr, hr)
        )
        scale = row_scale(i)
        co_ = jnp.concatenate([c4O[i], c4O[i]], axis=0)
        ch_ = jnp.concatenate([c4H[i], c4H[i]], axis=0)
        return co_ * o - scale * around_o, ch_ * h - (scale * side16) * around_h

    def once(i):
        o, h = apply_row(UO, UH, i)
        AO[i] = o
        AH[i] = h

    def twice(i):
        o, h = apply_row(AO, AH, i)
        FO[i - W] = o
        FH[i - W] = near(h)

    def lift(first, count):
        def body(n):
            row = first + n
            both = zcat[picks[row]]
            part = dot_nn(both, pb[row])
            LV[row] = part[0:cols] + part[cols:] + dot_nn(both[0:cols], pb2[row])

        loop(count, body, unroll=count)

    def leave(n):
        return pltpu.make_async_copy(
            r[("xst2", "rst2", "ust")[n]], r[("x_out", "r_out", "u_out")[n]], r["outsem"].at[n]
        )

    def stage(k, carry):
        def between():
            @pl.when(k > 0)
            def _():
                reduce_mid(k)

        local_solve(between)
        pack(VO, VH, sb.at[k])
        send_eight(sb.at[k], rb.at[k], exsem_s.at[1 + k], exsem_r.at[1 + k])

        @pl.when(k > 0)
        def _():
            dots_mid(k)

        @pl.when(k == 0)
        def _():
            for n in range(2):
                pltpu.make_async_copy(phr.at[n], phr.at[n], phsem_r.at[n]).wait()
            from_west = lax.rem(lane128, 8) < M4
            for half in range(2):
                value = jnp.where(from_west, has_w * phr[0, half, 0:128], has_e * phr[1, half, 0:128])
                high = value.astype(BF16)
                ph[half] = high
                ph2[half] = (value - high.astype(F32)).astype(BF16)
                pm[half] = jnp.where(from_west[0:8], phr[0, half, 128:136], phr[1, half, 128:136])
            assemble(cVO, csb, crb, exsem_r.at[1 + STAGES], take_coefficients)

        reduce_end(k)

        solved = jnp.zeros((cols, NCB * 128), F32)
        for m in range(NCB):
            both = halves(yw[m])
            part = dot_nn(both, bmat[m * 128 : (m + 1) * 128, :])
            solved = solved + part[0:cols] + part[cols:]
            solved = solved + dot_nn(both[0:cols], bmat2[m * 128 : (m + 1) * 128, :])
        for m in range(NCB):
            zcat[m] = halves(solved[:, m * 128 : (m + 1) * 128])
        lift(0, M4)
        lift(own - M4, M4)
        for half in range(2):
            total = zero
            for m in range(NCB):
                both = zcat[m]
                part = dot_nn(both, ph[half])
                part = part[0:cols] + part[cols:] + dot_nn(both[0:cols], ph2[half])
                total = total + part * jnp.broadcast_to(pm[half, m : m + 1, :], (cols, 128))
            pk[half] = total

        @pl.when(k < STAGES - 1)
        def _():
            for n in range(M4):
                nsb[k, n] = LV[n]
                nsb[k, M4 + 1 + n] = LV[own - M4 + n]
            nsb[k, M4] = pk[0]
            nsb[k, 2 * M4 + 1] = pk[1]
            for first, to, d in ((0, M4 + 1, -1), (M4 + 1, 0, 1)):
                pltpu.make_async_remote_copy(
                    src_ref=nsb.at[k, pl.ds(first, M4 + 1)],
                    dst_ref=nrb.at[k, pl.ds(to, M4 + 1)],
                    send_sem=nssem_s.at[k],
                    recv_sem=nssem_r.at[k],
                    device_id=(band_at(d), t),
                    device_id_type=MESH,
                ).start()

        lift(M4, own - 2 * M4)

        def keep(i, o, h):
            TO[i] = o
            TH[i] = h

        assemble(VO, sb.at[k], rb.at[k], exsem_r.at[1 + k], keep)

        @pl.when(k > 0)
        def _():
            g, d, e = dots_end(k)
            beta = jnp.where(k > 1, g / prev[0], 0.0)
            curv = jnp.where(k > 1, d + 2.0 * beta * e + beta * beta * prev[1], d)
            alpha = g / curv
            prev[0] = g
            prev[1] = curv
            prev[2] = alpha
            prev[3] = beta

            def body(row):
                p = UO[row + M4] + beta * Pp[row]
                s = FO[row + W] + beta * S[row]
                Pp[row] = p
                S[row] = s
                x_out[row] = x_out[row] + alpha * p
                r_out[row] = r_out[row] - alpha * s

            loop(own, body, unroll=own)

        @pl.when(k == STAGES - 1)
        def _():
            def body(row):
                r["xst2"][:, row, :] = x_out[row]
                r["rst2"][:, row, :] = r_out[row]

            loop(own, body, unroll=own)
            leave(0).start()
            leave(1).start()

        alpha = prev[2]
        beta = prev[3]

        def combine(i, o, h):
            ms = TO[i] + o + beta * MsO[i]
            MsO[i] = ms
            UO[i] = UO[i] - alpha * ms
            ms = TH[i] + h + beta * MsH[i]
            MsH[i] = ms
            UH[i] = UH[i] - alpha * ms

        for half, first_slot, first_row in ((0, M4, 0), (1, 0, 16 - M4)):
            strip = pk[half]

            def inner_rows(n):
                slot = first_slot + n
                h = pltpu.roll(strip, lax.rem(252 - 8 * slot, 128), 1) * side16
                combine(16 * half + slot, LV[first_row + n], h)

            loop(own // 2, inner_rows, unroll=own // 2)

        @pl.when(k < STAGES - 1)
        def _():
            loop(full - 10, lambda n: once(5 + n), unroll=full - 10)
            loop(full - 12, lambda n: twice(6 + n), unroll=full - 12)
            acc = restrict(2, own - 4, (zero,) * NCB)

            def dots(row, sums):
                u = UO[row + M4]
                return (
                    sums[0] + u * r_out[row],
                    sums[1] + u * FO[row + W],
                    sums[2] + u * S[row],
                )

            sums = loop(own - 4, lambda n, a: dots(2 + n, a), (zero, zero, zero), unroll=own - 4)

            pltpu.make_async_copy(nrb.at[k], nrb.at[k], nssem_r.at[k]).wait()
            for n in range(M4):
                combine(n, nrb[k, n] * has_n, pltpu.roll(nrb[k, M4], 60 - 8 * n, 1) * (has_n * side16))
                combine(
                    full - M4 + n,
                    nrb[k, M4 + 1 + n] * has_s,
                    pltpu.roll(nrb[k, 2 * M4 + 1], 92 - 8 * n, 1) * (has_s * side16),
                )
            for n in range(4):
                once(1 + n)
                once(full - 5 + n)
            for n in range(4):
                twice(2 + n)
                twice(full - 6 + n)
            acc = restrict(0, 2, acc)
            acc = restrict(own - 2, 2, acc)
            for m in range(NCB):
                qa[k + 1, m] = acc[m].astype(BF16)
            send_x(k + 1)

            for row in (0, 1, own - 2, own - 1):
                sums = dots(row, sums)
            dots_send(k + 1, *sums)

        @pl.when(k == STAGES - 1)
        def _():
            def body(row):
                r["ust"][:, row, :] = UO[row + M4]

            loop(own, body, unroll=own)
            leave(2).start()

        return carry

    lax.fori_loop(0, STAGES, stage, 0)

    pltpu.make_async_copy(irb, irb, exsem_s.at[0]).wait()
    pltpu.make_async_copy(crb, crb, exsem_s.at[1 + STAGES]).wait()

    def sent(e):
        pltpu.make_async_copy(rb.at[e], rb.at[e], exsem_s.at[1 + e]).wait()

    loop(STAGES, sent)
    for n in range(2):
        pltpu.make_async_copy(phr.at[n], phr.at[n], phsem_s.at[n]).wait()

    def sent_ns(k):
        pltpu.make_async_copy(nrb.at[k], nrb.at[k], nssem_s.at[k]).wait()

    loop(STAGES - 1, sent_ns)

    def sent_q(k):
        pltpu.make_async_copy(qar.at[k], qar.at[k], qasem_s.at[k]).wait()
        pltpu.make_async_copy(qbr.at[k], qbr.at[k], qbsem_s.at[k]).wait()

    loop(STAGES, sent_q)

    def sent_d(k):
        pltpu.make_async_copy(dar.at[k + 1], dar.at[k + 1], dasem_s.at[k + 1]).wait()
        pltpu.make_async_copy(dbr.at[k + 1], dbr.at[k + 1], dbsem_s.at[k + 1]).wait()

    loop(STAGES - 1, sent_d)
    for n in range(3):
        leave(n).wait()


def local(n_b, n_t, right_side, coeff_field, factor_blocks, block_rows, block_cols, prolong, coarse_picks, coarse_factor):
    cols, lat, lon = right_side.shape
    count = factor_blocks.shape[2]
    ext = lat + 2 * W
    full = lat + 2 * M4
    kt = (ext * (lon + 2 * W) + 127) // 128
    nx = 4 if n_t % 4 == 0 and n_t > 4 else 2
    nz = n_t // nx
    cfg = (n_b, n_t, nx, nz, lat, count, kt, cols)
    n_plane = n_b * nx - 1
    vm = pltpu.VMEM
    ext_f = vm((ext, cols, 128), F32)
    full_f = vm((full, cols, 128), F32)
    own_f = vm((lat, cols, 128), F32)
    cn = coarse_factor.shape[1:]
    four = vm((NCB, cols, 128), F32)
    dma = pltpu.SemaphoreType.DMA
    scratch = dict(
        tab=pltpu.SMEM((8, 128), jnp.int32),
        tabv=vm((8, 128), jnp.int32),
        lists=vm((8, 128), jnp.int32),
        br=vm((1, 1, count), jnp.int32),
        bc=vm((1, 1, count), jnp.int32),
        rs=vm((cols, lat, lon), F32),
        co=vm((lat, lon), F32),
        fac=vm((count, 128, 128), BF16),
        facT=vm((count, 128, 128), BF16),
        pf=vm((lat, 128, 128), F32),
        cf=vm(cn, F32),
        pb=vm((lat, 128, 128), BF16),
        pb2=vm((lat, 128, 128), BF16),
        bmat=vm(cn, BF16),
        bmat2=vm(cn, BF16),
        zcat=vm((NCB, 2 * cols, 128), BF16),
        iVO=ext_f,
        iVH=ext_f,
        isb=vm((24, cols, 128), F32),
        irb=vm((24, cols, 128), F32),
        cVO=vm((ext, 8, 128), F32),
        cVH=vm((ext, 8, 128), F32),
        csb=vm((24, 8, 128), F32),
        crb=vm((24, 8, 128), F32),
        VO=ext_f,
        VH=ext_f,
        sb=vm((STAGES, 24, cols, 128), F32),
        rb=vm((STAGES, 24, cols, 128), F32),
        LV=own_f,
        pk=vm((2, cols, 128), F32),
        nsb=vm((ITERS, 2 * M4 + 2, cols, 128), F32),
        nrb=vm((ITERS, 2 * M4 + 2, cols, 128), F32),
        pht=vm((2, 136, 128), F32),
        phr=vm((2, 2, 136, 128), F32),
        ph=vm((2, 128, 128), BF16),
        ph2=vm((2, 128, 128), BF16),
        pm=vm((2, 8, 128), F32),
        UO=full_f,
        UH=full_f,
        AO=full_f,
        AH=full_f,
        FO=ext_f,
        FH=ext_f,
        c4O=vm((full, 8, 128), F32),
        c4H=vm((full, 8, 128), F32),
        MsO=full_f,
        MsH=full_f,
        TO=full_f,
        TH=full_f,
        xst2=vm((cols, lat, 128), F32),
        rst2=vm((cols, lat, 128), F32),
        ust=vm((cols, lat, 128), F32),
        outsem=dma((3,)),
        xst=own_f,
        rst=own_f,
        S=own_f,
        Pp=own_f,
        yw=four,
        xin=vm((kt, cols, 128), BF16),
        gin=vm((kt, cols, 128), BF16),
        run=vm((count, cols, 128), F32),
        prev=vm((4, cols, 128), F32),
        qa=vm((STAGES, NCB, cols, 128), BF16),
        qar=vm((STAGES, nx - 1, NCB, cols, 128), BF16),
        qb=vm((STAGES, NCB, cols, 128), BF16),
        qbr=vm((STAGES, nz - 1, NCB, cols, 128), BF16),
        da=vm((STAGES, 8, 128), F32),
        dar=vm((STAGES, n_plane, 8, 128), F32),
        db=vm((STAGES, 8, 128), F32),
        dbr=vm((STAGES, nz - 1, 8, 128), F32),
        insem=dma((8,)),
        exsem_s=dma((2 + STAGES,)),
        exsem_r=dma((2 + STAGES,)),
        nssem_s=dma((ITERS,)),
        nssem_r=dma((ITERS,)),
        phsem_s=dma((2,)),
        phsem_r=dma((2,)),
    )
    for name in ("qasem_s", "qasem_r", "qbsem_s", "qbsem_r", "dasem_s", "dasem_r", "dbsem_s", "dbsem_r"):
        scratch[name] = dma((STAGES,))
    inputs = dict(
        picks=coarse_picks.reshape(lat),
        br_hbm=block_rows.reshape(1, 1, count),
        bc_hbm=block_cols.reshape(1, 1, count),
        rs_hbm=right_side,
        co_hbm=coeff_field,
        f_hbm=factor_blocks.reshape(factor_blocks.shape[2:]),
        p_hbm=prolong.reshape(lat, 128, lon),
        c_hbm=coarse_factor.reshape(cn),
    )
    results = ("x_out", "r_out", "u_out")
    out = jax.ShapeDtypeStruct((cols, lat, 128), F32)
    outs = pl.pallas_call(
        functools.partial(kernel, cfg, tuple(inputs) + results + tuple(scratch)),
        out_shape=(out, out, out),
        in_specs=[pl.BlockSpec(memory_space=pltpu.SMEM)]
        + [pl.BlockSpec(memory_space=pltpu.HBM)] * (len(inputs) - 1),
        out_specs=(pl.BlockSpec(memory_space=pltpu.HBM),) * 3,
        scratch_shapes=list(scratch.values()),
        compiler_params=pltpu.CompilerParams(
            collective_id=3, has_side_effects=True, vmem_limit_bytes=63 << 20
        ),
    )(*inputs.values())

    def hand_on(*refs):
        sems = refs[9]
        into = [pltpu.make_async_copy(refs[n], refs[6 + n], sems.at[n]) for n in range(3)]
        onto = [pltpu.make_async_copy(refs[6 + n], refs[3 + n], sems.at[3 + n]) for n in range(3)]
        for copy in into:
            copy.start()
        for n in range(3):
            into[n].wait()
            onto[n].start()
        for copy in onto:
            copy.wait()

    hbm = pl.BlockSpec(memory_space=pltpu.HBM)
    return pl.pallas_call(
        hand_on,
        out_shape=(out, out, out),
        in_specs=[hbm] * 3,
        out_specs=(hbm,) * 3,
        scratch_shapes=[vm(out.shape, F32)] * 3 + [dma((6,))],
        compiler_params=pltpu.CompilerParams(vmem_limit_bytes=63 << 20),
    )(*outs)


def solution(mesh):
    in_specs = (
        P(None, "band", "tile"),
        P("band", "tile"),
        P("band", "tile", None, None, None),
        P("band", "tile", None),
        P("band", "tile", None),
        P("band", None, None, "tile"),
        P("band", "tile", None),
        P("band", None, None),
    )
    out_specs = (P(None, "band", "tile"),) * 3
    return jax.shard_map(
        functools.partial(local, mesh.shape["band"], mesh.shape["tile"]),
        mesh=mesh,
        in_specs=in_specs,
        out_specs=out_specs,
        check_vma=False,
    )
```
